512 devices in a mesh: dp: 128 (over z, y, core), tensor: 4 (over x).
Axes of the slice: x: 4, y: 8, z: 8, core: 2. Of those that a mesh axis runs over, the one named last changes fastest.
Arguments:
- master: float32 [2, 8192, 2048], P(None, 'dp', 'tensor'), may hold values from -0.0625 to 0.0625
- momentum: float32 [2, 8192, 2048], P(None, 'dp', 'tensor'), may hold values from -6 to 6
- gradient: float32 [2, 8192, 2048], P(None, 'dp', 'tensor'), may hold values from -60 to 60
- bucket_table: int32 [4, 8], P('tensor'), may hold values from 0 to 3, as said below
- tokens: bfloat16 [32768, 8192], P('dp', 'tensor'), may hold values from -6 to 6
- norm_gain: float32 [8192], replicated, may hold values from 0.1 to 1.9
Outputs:
- new_master: float32 [2, 8192, 2048], P(None, 'dp', 'tensor')
- new_momentum: float32 [2, 8192, 2048], P(None, 'dp', 'tensor')
- key_values: bfloat16 [32768, 2048], P('dp', 'tensor')
The draws below stay inside these ranges and needn't reach their ends.
Inputs may be any that keep to these rules, and one draw needn't show every extreme that they name: `bucket_table`: in each row of 8 entries every value from 0 to 3 appears exactly twice.
All inputs are finite; a program needn't handle non-finite values.
Results may differ from the reference program's by a relative error of at most 0.001.
The reference program's roundings to bfloat16 on the way (of `normed` and `first_weights`) count: a program that leaves them out, or rounds other values in their place, can miss the bound.
Values may be sent and summed in bfloat16 or wider, within the bound.
A program may use at most 128 MiB of HBM per device.

```python
import math
import jax
import jax.numpy as jnp
from jax import lax

D = 8192
HD = 128
LAYERS = 2
NS_ITERS = 3
TOKENS = 32768
GROUPS = 4
MATS = 8
KVCOLS = 2048


def draw_gradient(key, part):
    key_list = jax.random.split(jax.random.fold_in(key, 11), 3)
    spread = math.log(10.0)
    row_scale = jnp.exp(jax.random.uniform(key_list[0], (LAYERS, D, 1), minval=-0.5 * spread, maxval=0.5 * spread))
    ramp_scale = (0.5 + jnp.arange(D, dtype=jnp.float32) / (D - 1)).reshape(1, D, 1)
    col_scale = jnp.exp(jax.random.uniform(key_list[1], (LAYERS, 1, KVCOLS), minval=-0.5 * spread, maxval=0.5 * spread))
    values = jax.random.truncated_normal(key_list[2], -4.0, 4.0, (LAYERS, D, KVCOLS), jnp.float32)
    return (values * row_scale * ramp_scale * col_scale).astype(jnp.float32)


def draw_bucket_table(key, part):
    group_keys = jax.random.split(jax.random.fold_in(key, 23), GROUPS)

    def one_group(group_key):
        order_ids = jax.random.permutation(group_key, MATS)
        position = jnp.argsort(order_ids)
        return (position // 2).astype(jnp.int32)
    return jax.vmap(one_group)(group_keys)


def steps_of(own_key, extent, shards, low, high):
    def one(dim, parts):
        draws = jax.random.uniform(jax.random.fold_in(jax.random.fold_in(own_key, 6), dim), (parts,), jnp.float32, low / len(shards), high / len(shards))
        return jnp.repeat(jnp.exp(draws), extent[dim] // parts).reshape((-1,) + (1,) * (len(extent) - dim - 1))

    level = one(*shards[0])
    for cut in shards[1:]:
        level = level * one(*cut)
    return level


def noise(key, dims, scale, bound, shards=(), held_as=jnp.bfloat16):
    array = jax.random.normal(key, dims, jnp.float32) * scale
    if len(shards) > 0:
        array = steps_of(key, dims, shards, -0.22, 0.18) * array
    return jnp.clip(array, min=-bound, max=bound).astype(held_as)


def setup_inputs(seed: int = 0) -> dict:
    seeds = jax.random.split(jax.random.key(seed), 7)
    master = noise(seeds[0], (LAYERS, D, KVCOLS), D ** -0.5, 0.0625, ((1, 128), (2, 4)), jnp.float32)
    momentum = noise(seeds[1], (LAYERS, D, KVCOLS), 1.0, 6.0, ((1, 128), (2, 4)), jnp.float32)
    gradient = draw_gradient(jax.random.fold_in(seeds[6], 71), 0)
    bucket_table = draw_bucket_table(jax.random.fold_in(seeds[6], 71), 0)
    tokens = noise(seeds[4], (TOKENS, D), 1.0, 6.0, ((0, 128), (1, 4)))
    norm_gain = jnp.clip(1.0 + 0.18 * jax.random.normal(seeds[5], (D,), jnp.float32), 0.1, 1.9)
    return {"master": master, "momentum": momentum, "gradient": gradient, "bucket_table": bucket_table, "tokens": tokens, "norm_gain": norm_gain}


beta_momentum = 0.95
learn_rate = 0.05
first_coeff = 3.4445
cube_coeff = -4.775
fifth_coeff = 2.0315
frob_epsilon = 1e-07
rms_epsilon = 1e-05

def reference(master, momentum, gradient, bucket_table, tokens, norm_gain):
    new_momentum = beta_momentum * momentum + gradient
    update = gradient + beta_momentum * new_momentum
    groups = bucket_table.shape[0]
    count = bucket_table.shape[1]
    slots = count // LAYERS
    heads = update.reshape(LAYERS, D, groups, slots, HD).transpose(2, 0, 3, 1, 4).reshape(groups, count, D, HD)
    sort_keys = bucket_table * count + jnp.arange(count, dtype=jnp.int32)[None, :]
    order_ids = jnp.argsort(sort_keys, axis=1).astype(jnp.int32)
    picked = jnp.take_along_axis(heads, order_ids[:, :, None, None], axis=1)
    stacked = picked.reshape(groups, count // 2, 2, D, HD).transpose(0, 1, 3, 2, 4).reshape(groups, count // 2, D, 2 * HD)
    norms = jnp.sqrt(lax.optimization_barrier(jnp.sum(stacked * stacked, axis=(2, 3))))
    current = stacked / (norms + frob_epsilon)[:, :, None, None]
    for iteration in range(NS_ITERS):
        gram_mat = jnp.einsum('gbdk,gbdj->gbkj', current, current, precision=lax.Precision.HIGHEST)
        square = jnp.einsum('gbkj,gbjl->gbkl', gram_mat, gram_mat, precision=lax.Precision.HIGHEST)
        factor = cube_coeff * gram_mat + fifth_coeff * square
        current = first_coeff * current + jnp.einsum('gbdk,gbkj->gbdj', current, factor, precision=lax.Precision.HIGHEST)
    split = current.reshape(groups, count // 2, D, 2, HD).transpose(0, 1, 3, 2, 4).reshape(groups, count, D, HD)
    inverse = jnp.argsort(order_ids, axis=1).astype(jnp.int32)
    restored = jnp.take_along_axis(split, inverse[:, :, None, None], axis=1)
    ortho = restored.reshape(groups, LAYERS, slots, D, HD).transpose(1, 3, 0, 2, 4).reshape(LAYERS, D, groups * slots * HD)
    step_scale = learn_rate * math.sqrt(max(1.0, D / (2.0 * HD)))
    new_master = master - step_scale * ortho
    tokens_f = tokens.astype(jnp.float32)
    inv_rms = lax.rsqrt(lax.optimization_barrier(jnp.mean(tokens_f * tokens_f, axis=1, keepdims=True)) + rms_epsilon)
    normed = (tokens_f * inv_rms * norm_gain[None, :]).astype(jnp.bfloat16)
    first_weights = new_master[0].astype(jnp.bfloat16)
    key_values = jnp.dot(normed, first_weights, preferred_element_type=jnp.float32).astype(jnp.bfloat16)
    return (new_master, new_momentum, key_values)
```

```python
import functools
import math

import jax
import jax.numpy as jnp
from jax import lax
from jax.experimental import pallas as pl
from jax.experimental.pallas import tpu as pltpu
from jax.sharding import Mesh
from jax.sharding import PartitionSpec as P

HD = 128
NS_ITERS = 3
DP = ("dp_0", "dp_1", "dp_2")

beta_momentum = 0.95
learn_rate = 0.05
first_coeff = 3.4445
cube_coeff = -4.775
fifth_coeff = 2.0315
frob_epsilon = 1e-07
rms_epsilon = 1e-05

F32 = jnp.float32
BF16 = jnp.bfloat16
Y, Z, C, X = "dp_1", "dp_0", "dp_2", "tensor"
PACKED = 3 * HD


def near_first(n):
    offsets = [0]
    for k in range(1, n // 2):
        offsets += [k, -k]
    return [*offsets, n // 2]


def split(a):
    high = a.astype(BF16)
    return high, (a - high.astype(F32)).astype(BF16)


def dot(a, b):
    return jnp.dot(a, b, preferred_element_type=F32)


def dot3(a, b):
    return dot(a[0], b[0]) + (dot(a[0], b[1]) + dot(a[1], b[0]))


def kernel(n, d_model, table, master, momentum, gradient, tokens, gain, new_master, new_momentum,
           key_values, update, stacked, other_rows, heads, other_heads, packed, came1, part, came2,
           gram, ortho, weights, came_tokens, squares, normed, total, kv_send, kv_blocks,
           pair_send, pair_recv, gram_send, gram_recv, token_send, token_recv, first_send,
           first_recv, ring_send, ring_recv):
    half = n // 2
    rows = PACKED // n
    count = tokens.shape[0]
    blocks = tokens.shape[1] // HD
    height = master.shape[1]
    z, y, c, x = (lax.axis_index(a) for a in (Z, Y, C, X))
    axes = ((Y, Z), (Z, Y))
    place = {Y: y, Z: z}
    pending = []

    def at(axis, offset, size):
        here = {Y: y, Z: z, X: x}[axis]
        return lax.rem(here + (offset + size), size)

    def send(src, dst, sems, to):
        copy = pltpu.make_async_remote_copy(
            src_ref=src, dst_ref=dst, send_sem=sems[0], recv_sem=sems[1],
            device_id=to, device_id_type=pl.DeviceIdType.MESH,
        )
        copy.start()
        pending.append(copy)

    def arrived(ref, sems, to):
        pltpu.make_async_remote_copy(
            src_ref=ref, dst_ref=ref, send_sem=sems[0], recv_sem=sems[1],
            device_id=to, device_id_type=pl.DeviceIdType.MESH,
        ).wait_recv()

    def finish_sends():
        while pending:
            pending.pop(0).wait_send()

    partner = {C: 1 - c}

    barrier = pltpu.get_barrier_semaphore()
    greeted = [partner, {X: at(X, 1, 4)}, {X: at(X, -1, 4)}]
    for axis in (Y, Z):
        greeted += [{axis: at(axis, d, n)} for d in range(1, n)]
    for device in greeted:
        pl.semaphore_signal(barrier, inc=1, device_id=device, device_id_type=pl.DeviceIdType.MESH)

    bucket = [table[0, i] for i in range(8)]
    position = []
    for i in range(8):
        earlier = jnp.int32(0)
        for j in range(i):
            earlier += jnp.where(bucket[j] == bucket[i], 1, 0)
        position.append(2 * bucket[i] + earlier)
    held = []
    for s in range(8):
        which = jnp.int32(0)
        for i in range(8):
            which += jnp.where(position[i] == s, i, 0)
        held.append(which)

    for layer in range(2):
        for slot in range(4):
            lanes = slice(slot * HD, (slot + 1) * HD)
            g = gradient[layer, :, lanes]
            m = beta_momentum * momentum[layer, :, lanes] + g
            new_momentum[layer, :, lanes] = m
            update[layer * 4 + slot] = g + beta_momentum * m
            if layer == 0:
                heads[slot] = master[0, :, lanes]
    for s in range(8):
        stacked[s] = update[held[s]]

    pl.semaphore_wait(barrier, len(greeted))

    def pair(k):
        return pair_send.at[k], pair_recv.at[k]

    send(stacked.at[pl.ds(4 * (1 - c), 4)], other_rows, pair(0), partner)
    send(heads.at[pl.ds(2 * (1 - c), 2)], other_heads, pair(1), partner)

    right, left = {X: at(X, 1, 4)}, {X: at(X, -1, 4)}
    upper, lower = pl.ds(0, count // 2), pl.ds(count // 2, count // 2)

    def tok(k):
        return token_send.at[k], token_recv.at[k]

    send(tokens.at[upper], came_tokens.at[0, upper], tok(0), right)
    send(tokens.at[lower], came_tokens.at[2, lower], tok(1), left)
    send(tokens.at[lower], came_tokens.at[0, lower], tok(2), right)
    send(tokens.at[upper], came_tokens.at[2, upper], tok(3), left)

    arrived(other_rows, pair(0), partner)

    def chip_rows(b):
        own = jnp.concatenate([stacked[4 * c + 2 * b], stacked[4 * c + 2 * b + 1]], axis=1)
        other = jnp.concatenate([other_rows[2 * b], other_rows[2 * b + 1]], axis=1)
        return jnp.concatenate([own, other], axis=0)

    def lines(ref, net, chunk):
        return ref.at[net, pl.ds(pl.multiple_of(chunk * rows, 8), rows)]

    def gsem(stage, net, d):
        return gram_send.at[stage, net, d - 1], gram_recv.at[stage, net, d - 1]

    for net in range(2):
        s = chip_rows(net)
        g = dot3(split(s.T), split(s))
        packed[net, 0:HD] = g[:HD, :HD]
        packed[net, HD : 2 * HD] = g[:HD, HD:]
        packed[net, 2 * HD : 3 * HD] = g[HD:, HD:]
        axis = axes[net][0]
        for d in range(1, n):
            to = at(axis, d, n)
            send(lines(packed, net, to), came1.at[net, d - 1], gsem(0, net, d), {axis: to})

    def add_squares(src, fresh):
        tile = 32 if count % 32 == 0 else 16

        def body(i, _):
            r = pl.ds(pl.multiple_of(i * tile, tile), tile)
            t = jnp.zeros((tile, HD), F32) if fresh else squares[r]
            for j in range(blocks):
                v = src[r, j * HD : (j + 1) * HD].astype(F32)
                t = t + v * v
            squares[r] = t
            return 0

        lax.fori_loop(0, count // tile, body, 0)

    add_squares(tokens, True)

    for net in range(2):
        axis, other = axes[net]
        for d in range(1, n):
            arrived(came1.at[net, d - 1], gsem(0, net, d), {axis: at(axis, d, n)})
        s = packed[net, pl.ds(pl.multiple_of(place[axis] * rows, 8), rows)]
        for d in range(1, n):
            s = s + came1[net, d - 1]
        part[net] = s
        for d in range(1, n):
            send(part.at[net], came2.at[net, d - 1], gsem(1, net, d), {other: at(other, d, n)})
    for net in range(2):
        axis, other = axes[net]
        for d in range(1, n):
            arrived(came2.at[net, d - 1], gsem(1, net, d), {other: at(other, d, n)})
        s = part[net]
        for d in range(1, n):
            s = s + came2[net, d - 1]
        gram[net, pl.ds(pl.multiple_of(place[axis] * rows, 8), rows)] = s
        own = lines(gram, net, place[axis])
        for d in range(1, n):
            send(own, own, gsem(2, net, d), {axis: at(axis, d, n)})

    arrived(came_tokens.at[0, upper], tok(0), right)
    send(came_tokens.at[0, upper], came_tokens.at[1, upper], tok(4), right)
    arrived(came_tokens.at[2, lower], tok(1), left)
    send(came_tokens.at[2, lower], came_tokens.at[1, lower], tok(5), left)

    for net in range(2):
        axis = axes[net][0]
        for d in range(1, n):
            arrived(lines(gram, net, at(axis, -d, n)), gsem(2, net, d), {axis: at(axis, d, n)})

    r_id = lax.broadcasted_iota(jnp.int32, (2 * HD, 2 * HD), 0)
    c_id = lax.broadcasted_iota(jnp.int32, (2 * HD, 2 * HD), 1)
    eye = jnp.where(r_id == c_id, 1.0, 0.0).astype(F32)
    grams, scales, products = [], [], [None, None]
    for net in range(2):
        corner = gram[net, HD : 2 * HD]
        top = jnp.concatenate([gram[net, 0:HD], corner], axis=1)
        bottom = jnp.concatenate([corner.T, gram[net, 2 * HD : 3 * HD]], axis=1)
        g = jnp.concatenate([top, bottom], axis=0)
        trace = jnp.sum(jnp.sum(g * eye, axis=1, keepdims=True), axis=0, keepdims=True)
        scale = 1.0 / (jnp.sqrt(trace) + frob_epsilon)
        grams.append(g * (scale * scale))
        scales.append(scale)
    for iteration in range(NS_ITERS):
        gs = [split(g) for g in grams]
        squared = [dot3(g, g) for g in gs]
        factor = [
            first_coeff * eye + (cube_coeff * g + fifth_coeff * q) for g, q in zip(grams, squared)
        ]
        fs = [split(f) for f in factor]
        if iteration == 0:
            products = factor
        else:
            products = [dot3(split(p), f) for p, f in zip(products, fs)]
        if iteration + 1 < NS_ITERS:
            half_way = [dot3(f, g) for f, g in zip(fs, gs)]
            grams = [dot3(split(h), f) for h, f in zip(half_way, fs)]

    step = learn_rate * math.sqrt(max(1.0, d_model / (2.0 * HD)))
    for net in range(2):
        moved = dot3(split(chip_rows(net)), split(products[net] * (scales[net] * step)))
        for h in range(2):
            lanes = slice(h * HD, (h + 1) * HD)
            ortho[4 * c + 2 * net + h, c] = moved[:height, lanes]
            ortho[4 * c + 2 * net + h, 1 - c] = moved[height:, lanes]
    mine = ortho.at[pl.ds(4 * c, 4)]
    send(mine, mine, pair(2), partner)
    arrived(other_heads, pair(1), partner)
    arrived(ortho.at[pl.ds(4 * (1 - c), 4)], pair(2), partner)

    order = near_first(n)
    slot_of = {o % n: k for k, o in enumerate(order)}
    ring_axis = (Z, Y)

    def fsem(net, d):
        return first_send.at[net, d - 1], first_recv.at[net, d - 1]

    for net in range(2):
        where = jnp.where(c == 0, position[net], position[2 + net])
        block = place[ring_axis[net]]
        weights[net, block, 0, c] = (heads[2 * c + net] - ortho[where, c]).astype(BF16)
        weights[net, block, 0, 1 - c] = (other_heads[net] - ortho[where, 1 - c]).astype(BF16)
        axis = axes[net][0]
        for o in order[1:]:
            d = o % n
            send(weights.at[net, block, 0], weights.at[net, block, slot_of[-o % n]], fsem(net, d),
                 {axis: at(axis, d, n)})

    for i in range(8):
        lanes = slice((i % 4) * HD, (i % 4 + 1) * HD)
        new_master[i // 4, :, lanes] = master[i // 4, :, lanes] - ortho[position[i], c]

    def first_came(net, group):
        axis = axes[net][0]
        for k in range(max(1, group * half), (group + 1) * half):
            d = -order[k] % n
            arrived(weights.at[net, place[ring_axis[net]], k], fsem(net, d), {axis: at(axis, d, n)})

    def rsem(net, way, s, h):
        return ring_send.at[net, way, s, h], ring_recv.at[net, way, s, h]

    def sub(net, offset, h):
        return weights.at[net, at(ring_axis[net], offset, n), pl.ds(h * half, half)]

    def goes(way, s, h):
        return s + 1 < half or way == h

    seen = set()

    def need(net, way, s, h):
        if (net, way, s, h) in seen or not goes(way, s, h):
            return
        seen.add((net, way, s, h))
        sign = 1 if way == 0 else -1
        arrived(sub(net, -sign * (s + 1), h), rsem(net, way, s, h),
                {ring_axis[net]: at(ring_axis[net], sign, n)})

    def ring(s, h):
        for net in range(2):
            if s == 0:
                first_came(net, h)
            for way in range(2):
                if s > 0:
                    if not goes(way, s, h):
                        continue
                    need(net, way, s - 1, h)
                if goes(way, s, h):
                    sign = 1 if way == 0 else -1
                    moving = sub(net, -sign * s, h)
                    send(moving, moving, rsem(net, way, s, h),
                         {ring_axis[net]: at(ring_axis[net], sign, n)})

    def inverse_rms():
        mean = jnp.sum(squares[...], axis=1, keepdims=True) / d_model
        squares[...] = jnp.broadcast_to(lax.rsqrt(mean + rms_epsilon), squares.shape)

    def normalise(src, offset, k):
        tile = 32 if count % 32 == 0 else 16
        first = at(X, offset, 4) * blocks

        def body(i, _):
            r = pl.ds(pl.multiple_of(i * tile, tile), tile)
            inverse = squares[r]
            for j in range(blocks):
                v = src[r, j * HD : (j + 1) * HD].astype(F32)
                v = v * inverse * gain[pl.ds(first + j, 1), :]
                normed[first + j, c, r] = v.astype(BF16)
            return 0

        lax.fori_loop(0, count // tile, body, 0)
        made = normed.at[pl.ds(first, blocks), c]
        send(made, made, pair(3 + k), partner)

    def partner_normed(offset, k):
        first = at(X, offset, 4) * blocks
        arrived(normed.at[pl.ds(first, blocks), 1 - c], pair(3 + k), partner)

    def multiply(net, offset, fresh=False):
        block = at(ring_axis[net], offset, n)
        axis = axes[net][0]
        wide = []
        for o in order:
            across = at(axis, o, n)
            feature = block * n + across if net == 0 else across * n + block
            wide.append(normed[feature].reshape(2 * count, HD))
        product = dot(jnp.concatenate(wide, axis=1), weights[net, block].reshape(n * HD, HD))
        total[net] = product if fresh else total[net] + product

    def tokens_one():
        arrived(came_tokens.at[0, lower], tok(2), right)
        add_squares(came_tokens.at[0], False)

    def tokens_three():
        arrived(came_tokens.at[2, upper], tok(3), left)
        add_squares(came_tokens.at[2], False)

    def tokens_two():
        arrived(came_tokens.at[1, upper], tok(4), right)
        arrived(came_tokens.at[1, lower], tok(5), left)
        add_squares(came_tokens.at[1], False)
        inverse_rms()

    def own_block():
        for k, offset in enumerate((0, -1, 1, 2)):
            partner_normed(offset, k)
        for net in range(2):
            multiply(net, 0, True)

    def distance(k):
        for net in range(2):
            for h in range(2):
                for way in range(2):
                    need(net, way, k - 1, h)
            multiply(net, k)
            if k < half:
                multiply(net, -k)

    work = [
        [tokens_one],
        [tokens_three, tokens_two],
        [lambda: normalise(tokens, 0, 0), lambda: normalise(came_tokens.at[0], -1, 1)],
        [lambda: normalise(came_tokens.at[2], 1, 2), lambda: normalise(came_tokens.at[1], 2, 3)],
        [own_block],
        [functools.partial(distance, 1)],
    ]
    work += [[functools.partial(distance, k)] for k in range(2, half + 1)]
    for s in range(half):
        for h in range(2):
            ring(s, h)
            if s + 1 == half and half > 1 and h == 0:
                continue
            for task in work.pop(0):
                task()
    for tasks in work:
        for task in tasks:
            task()

    for net in range(2):
        kv_send[net] = total[net, pl.ds(pl.multiple_of((1 - c) * count, 16), count)].astype(BF16)
    send(kv_send, kv_blocks.at[pl.ds(2 * c, 2)], pair(7), partner)
    for net in range(2):
        kv_blocks[2 * c + net] = total[net, pl.ds(pl.multiple_of(c * count, 16), count)].astype(BF16)
    arrived(kv_blocks.at[pl.ds(2 * (1 - c), 2)], pair(7), partner)
    for k in range(4):
        key_values[:, k * HD : (k + 1) * HD] = kv_blocks[k]
    finish_sends()


def per_device(n, d_model, master, momentum, gradient, bucket_table, tokens, norm_gain):
    height = master.shape[1]
    count, width = tokens.shape
    blocks = width // HD
    rows = PACKED // n
    half = n // 2
    vmem = pl.BlockSpec(memory_space=pltpu.VMEM)
    dma = pltpu.SemaphoreType.DMA
    scratch = [
        pltpu.VMEM((8, height, HD), F32),
        pltpu.VMEM((8, height, HD), F32),
        pltpu.VMEM((4, height, HD), F32),
        pltpu.VMEM((4, height, HD), F32),
        pltpu.VMEM((2, height, HD), F32),
        pltpu.VMEM((2, PACKED, HD), F32),
        pltpu.VMEM((2, n - 1, rows, HD), F32),
        pltpu.VMEM((2, rows, HD), F32),
        pltpu.VMEM((2, n - 1, rows, HD), F32),
        pltpu.VMEM((2, PACKED, HD), F32),
        pltpu.VMEM((8, 2, height, HD), F32),
        pltpu.VMEM((2, n, n, 2, height, HD), BF16),
        pltpu.VMEM((3, count, width), BF16),
        pltpu.VMEM((count, HD), F32),
        pltpu.VMEM((4 * blocks, 2, count, HD), BF16),
        pltpu.VMEM((2, 2 * count, HD), F32),
        pltpu.VMEM((2, count, HD), BF16),
        pltpu.VMEM((4, count, HD), BF16),
        dma((8,)),
        dma((8,)),
        dma((3, 2, n - 1)),
        dma((3, 2, n - 1)),
        dma((6,)),
        dma((6,)),
        dma((2, n - 1)),
        dma((2, n - 1)),
        dma((2, 2, half, 2)),
        dma((2, 2, half, 2)),
    ]
    return pl.pallas_call(
        functools.partial(kernel, n, d_model),
        out_shape=(
            jax.ShapeDtypeStruct(master.shape, F32),
            jax.ShapeDtypeStruct(master.shape, F32),
            jax.ShapeDtypeStruct((count, 4 * HD), BF16),
        ),
        in_specs=[pl.BlockSpec(memory_space=pltpu.SMEM), vmem, vmem, vmem, vmem, vmem],
        out_specs=(vmem, vmem, vmem),
        scratch_shapes=scratch,
        compiler_params=pltpu.CompilerParams(
            collective_id=0, has_side_effects=True, vmem_limit_bytes=48 * 1024 * 1024
        ),
    )(bucket_table, master, momentum, gradient, tokens, norm_gain.reshape(-1, HD))


def solution(mesh):
    n = math.isqrt(mesh.shape["dp"] // 2)
    torus = Mesh(
        mesh.devices.reshape(n, n, 2, mesh.shape["tensor"]), ("dp_0", "dp_1", "dp_2", "tensor")
    )

    def whole(*args):
        return jax.shard_map(
            functools.partial(per_device, n, args[0].shape[1]),
            mesh=torus,
            in_specs=(
                P(None, DP, "tensor"),
                P(None, DP, "tensor"),
                P(None, DP, "tensor"),
                P("tensor", None),
                P(DP, "tensor"),
                P(),
            ),
            out_specs=(P(None, DP, "tensor"), P(None, DP, "tensor"), P(DP, "tensor")),
            check_vma=False,
        )(*args)

    return whole
```

```python
import functools
import math

import jax
import jax.numpy as jnp
from jax import lax
from jax.experimental import pallas as pl
from jax.experimental.pallas import tpu as pltpu
from jax.sharding import Mesh
from jax.sharding import PartitionSpec as P

HD = 128
NS_ITERS = 3
DP = ("dp_0", "dp_1", "dp_2")

beta_momentum = 0.95
learn_rate = 0.05
first_coeff = 3.4445
cube_coeff = -4.775
fifth_coeff = 2.0315
frob_epsilon = 1e-07
rms_epsilon = 1e-05

F32 = jnp.float32
BF16 = jnp.bfloat16
Y, Z, C, X = "dp_1", "dp_0", "dp_2", "tensor"
PACKED = 2 * HD + 64


def near_first(n):
    offsets = [0]
    for k in range(1, n // 2):
        offsets += [k, -k]
    return [*offsets, n // 2]


def split(a):
    high = a.astype(BF16)
    return high, (a - high.astype(F32)).astype(BF16)


def dot(a, b):
    return jnp.dot(a, b, preferred_element_type=F32)


def dot3(a, b):
    return dot(a[0], b[0]) + (dot(a[0], b[1]) + dot(a[1], b[0]))


def kernel(n, d_model, table_in, master_in, momentum_in, gradient_in, tokens_in, gain_in, new_master,
           new_momentum, key_values, table, master, momentum, gradient, tokens, gain, load, store, update,
           stacked, other_rows, heads, other_heads, packed, came1, part, came2, gram, ortho, weights,
           came_tokens, squares, normed, total, kv_send, kv_blocks, pair_send, pair_recv, gram_send,
           gram_recv, token_send, token_recv, first_send, first_recv, begin_send, begin_recv, ring_send,
           ring_recv):
    half = n // 2
    rows = PACKED // n
    count = tokens.shape[0]
    blocks = tokens.shape[1] // HD
    height = master.shape[1]
    z, y, c, x = (lax.axis_index(a) for a in (Z, Y, C, X))
    axes = ((Y, Z), (Z, Y))
    place = {Y: y, Z: z}
    pending = []

    def at(axis, offset, size):
        here = {Y: y, Z: z, X: x}[axis]
        return lax.rem(here + (offset + size), size)

    def send(src, dst, sems, to):
        copy = pltpu.make_async_remote_copy(
            src_ref=src, dst_ref=dst, send_sem=sems[0], recv_sem=sems[1],
            device_id=to, device_id_type=pl.DeviceIdType.MESH,
        )
        copy.start()
        pending.append(copy)

    def arrived(ref, sems, to):
        pltpu.make_async_remote_copy(
            src_ref=ref, dst_ref=ref, send_sem=sems[0], recv_sem=sems[1],
            device_id=to, device_id_type=pl.DeviceIdType.MESH,
        ).wait_recv()

    def finish_sends():
        while pending:
            pending.pop(0).wait_send()

    partner = {C: 1 - c}

    barrier = pltpu.get_barrier_semaphore()
    greeted = [partner, {X: at(X, 1, 4)}, {X: at(X, -1, 4)}]
    for axis in (Y, Z):
        greeted += [{axis: at(axis, d, n)} for d in range(1, n)]
    for device in greeted:
        pl.semaphore_signal(barrier, inc=1, device_id=device, device_id_type=pl.DeviceIdType.MESH)

    loads = [
        pltpu.make_async_copy(src, dst, load.at[k])
        for k, (src, dst) in enumerate((
            (table_in, table), (gradient_in, gradient), (momentum_in, momentum),
            (master_in, master), (tokens_in, tokens), (gain_in, gain),
        ))
    ]
    for copy in loads:
        copy.start()
    loads[0].wait()

    bucket = [table[0, i] for i in range(8)]
    position = []
    for i in range(8):
        earlier = jnp.int32(0)
        for j in range(i):
            earlier += jnp.where(bucket[j] == bucket[i], 1, 0)
        position.append(2 * bucket[i] + earlier)
    held = []
    for s in range(8):
        which = jnp.int32(0)
        for i in range(8):
            which += jnp.where(position[i] == s, i, 0)
        held.append(which)

    for copy in loads[1:4]:
        copy.wait()
    for layer in range(2):
        for slot in range(4):
            lanes = slice(slot * HD, (slot + 1) * HD)
            g = gradient[layer, :, lanes]
            m = beta_momentum * momentum[layer, :, lanes] + g
            momentum[layer, :, lanes] = m
            update[layer * 4 + slot] = g + beta_momentum * m
            if layer == 0:
                heads[slot] = master[0, :, lanes]
    for s in range(8):
        stacked[s] = update[held[s]]
    stores = [pltpu.make_async_copy(momentum, new_momentum, store.at[0])]
    stores[0].start()

    pl.semaphore_wait(barrier, len(greeted))

    def pair(k):
        return pair_send.at[k], pair_recv.at[k]

    send(stacked.at[pl.ds(4 * (1 - c), 4)], other_rows, pair(0), partner)
    send(heads.at[pl.ds(2 * (1 - c), 2)], other_heads, pair(1), partner)

    right, left = {X: at(X, 1, 4)}, {X: at(X, -1, 4)}
    upper, lower = pl.ds(0, count // 2), pl.ds(count // 2, count // 2)

    for copy in loads[4:]:
        copy.wait()

    def tok(k):
        return token_send.at[k], token_recv.at[k]

    send(tokens.at[upper], came_tokens.at[0, upper], tok(0), right)
    send(tokens.at[lower], came_tokens.at[2, lower], tok(1), left)
    send(tokens.at[lower], came_tokens.at[0, lower], tok(2), right)
    send(tokens.at[upper], came_tokens.at[2, upper], tok(3), left)

    arrived(other_rows, pair(0), partner)

    def chip_rows(b):
        own = jnp.concatenate([stacked[4 * c + 2 * b], stacked[4 * c + 2 * b + 1]], axis=1)
        other = jnp.concatenate([other_rows[2 * b], other_rows[2 * b + 1]], axis=1)
        return jnp.concatenate([own, other], axis=0)

    def lines(ref, net, chunk):
        return ref.at[net, pl.ds(pl.multiple_of(chunk * rows, 8), rows)]

    far_first = [o % n for o in reversed(near_first(n)[1:])]

    def gsem(stage, net, d):
        return gram_send.at[stage, net, d - 1], gram_recv.at[stage, net, d - 1]

    r_id = lax.broadcasted_iota(jnp.int32, (HD, HD), 0)
    c_id = lax.broadcasted_iota(jnp.int32, (HD, HD), 1)
    for net in range(2):
        s = chip_rows(net)
        g = dot3(split(s.T), split(s))
        second = g[HD:, HD:]
        packed[net, 0:HD] = jnp.where(r_id <= c_id, g[:HD, :HD], second)
        packed[net, HD : 2 * HD] = g[:HD, HD:]
        diagonal = jnp.sum(jnp.where(r_id == c_id, second, 0.0), axis=0, keepdims=True)
        packed[net, 2 * HD :] = jnp.broadcast_to(diagonal, (PACKED - 2 * HD, HD))
        axis = axes[net][0]
        for d in far_first:
            to = at(axis, d, n)
            send(lines(packed, net, to), came1.at[net, d - 1], gsem(0, net, d), {axis: to})

    def add_squares(src, fresh):
        tile = 32 if count % 32 == 0 else 16

        def body(i, _):
            r = pl.ds(pl.multiple_of(i * tile, tile), tile)
            t = jnp.zeros((tile, HD), F32) if fresh else squares[r]
            for j in range(blocks):
                v = src[r, j * HD : (j + 1) * HD].astype(F32)
                t = t + v * v
            squares[r] = t
            return 0

        lax.fori_loop(0, count // tile, body, 0)

    add_squares(tokens, True)

    for net in range(2):
        axis, other = axes[net]
        for d in range(1, n):
            arrived(came1.at[net, d - 1], gsem(0, net, d), {axis: at(axis, d, n)})
        s = packed[net, pl.ds(pl.multiple_of(place[axis] * rows, 8), rows)]
        for d in range(1, n):
            s = s + came1[net, d - 1]
        part[net] = s
        for d in far_first:
            send(part.at[net], came2.at[net, d - 1], gsem(1, net, d), {other: at(other, d, n)})
    for net in range(2):
        axis, other = axes[net]
        for d in range(1, n):
            arrived(came2.at[net, d - 1], gsem(1, net, d), {other: at(other, d, n)})
        s = part[net]
        for d in range(1, n):
            s = s + came2[net, d - 1]
        gram[net, pl.ds(pl.multiple_of(place[axis] * rows, 8), rows)] = s
        own = lines(gram, net, place[axis])
        for d in far_first:
            send(own, own, gsem(2, net, d), {axis: at(axis, d, n)})

    arrived(came_tokens.at[0, upper], tok(0), right)
    send(came_tokens.at[0, upper], came_tokens.at[1, upper], tok(4), right)
    arrived(came_tokens.at[2, lower], tok(1), left)
    send(came_tokens.at[2, lower], came_tokens.at[1, lower], tok(5), left)

    for net in range(2):
        axis = axes[net][0]
        for d in range(1, n):
            arrived(lines(gram, net, at(axis, -d, n)), gsem(2, net, d), {axis: at(axis, d, n)})

    eye = jnp.where(
        lax.broadcasted_iota(jnp.int32, (2 * HD, 2 * HD), 0)
        == lax.broadcasted_iota(jnp.int32, (2 * HD, 2 * HD), 1), 1.0, 0.0
    ).astype(F32)
    grams, scales, products = [], [], [None, None]
    for net in range(2):
        both, corner = gram[net, 0:HD], gram[net, HD : 2 * HD]
        turned = both.T
        one = jnp.where(r_id <= c_id, both, turned)
        two = jnp.where(r_id > c_id, both, jnp.where(r_id < c_id, turned, gram[net, 2 * HD : 2 * HD + 1]))
        top = jnp.concatenate([one, corner], axis=1)
        bottom = jnp.concatenate([corner.T, two], axis=1)
        g = jnp.concatenate([top, bottom], axis=0)
        trace = jnp.sum(jnp.sum(g * eye, axis=1, keepdims=True), axis=0, keepdims=True)
        scale = 1.0 / (jnp.sqrt(trace) + frob_epsilon)
        grams.append(g * (scale * scale))
        scales.append(scale)
    for iteration in range(NS_ITERS):
        gs = [split(g) for g in grams]
        squared = [dot3(g, g) for g in gs]
        factor = [
            first_coeff * eye + (cube_coeff * g + fifth_coeff * q) for g, q in zip(grams, squared)
        ]
        fs = [split(f) for f in factor]
        if iteration == 0:
            products = factor
        else:
            products = [dot3(split(p), f) for p, f in zip(products, fs)]
        if iteration + 1 < NS_ITERS:
            half_way = [dot3(f, g) for f, g in zip(fs, gs)]
            grams = [dot3(split(h), f) for h, f in zip(half_way, fs)]

    step = learn_rate * math.sqrt(max(1.0, d_model / (2.0 * HD)))
    for net in range(2):
        moved = dot3(split(chip_rows(net)), split(products[net] * (scales[net] * step)))
        for h in range(2):
            lanes = slice(h * HD, (h + 1) * HD)
            ortho[4 * c + 2 * net + h, c] = moved[:height, lanes]
            ortho[4 * c + 2 * net + h, 1 - c] = moved[height:, lanes]
    mine = ortho.at[pl.ds(4 * c, 4)]
    send(mine, mine, pair(2), partner)
    arrived(other_heads, pair(1), partner)
    arrived(ortho.at[pl.ds(4 * (1 - c), 4)], pair(2), partner)

    order = near_first(n)
    slot_of = {o % n: k for k, o in enumerate(order)}
    ring_axis = (Z, Y)

    def rsem(net, way, s, h):
        return ring_send.at[net, way, s, h], ring_recv.at[net, way, s, h]

    def bsem(net, way, k):
        return begin_send.at[net, way, k], begin_recv.at[net, way, k]

    def fsem(net, k):
        return first_send.at[net, k], first_recv.at[net, k]

    def sub(net, offset, h):
        return weights.at[net, at(ring_axis[net], offset, n), pl.ds(h * half, half)]

    def piece(net, offset, k):
        return weights.at[net, at(ring_axis[net], offset, n), k]

    def goes(way, s, h):
        return s + 1 < half or way == h

    def pass_on(net, j):
        axis = axes[net][0]
        if j + 1 < half:
            for sign in (1, -1):
                k = slot_of[sign * (j + 1) % n]
                send(piece(net, 0, slot_of[sign * j % n]), piece(net, 0, k), fsem(net, k),
                     {axis: at(axis, -sign, n)})
        elif j + 1 == half:
            k = slot_of[half]
            source = jnp.where(c == 0, slot_of[j % n], slot_of[-j % n])
            send(piece(net, 0, source), piece(net, 0, k), fsem(net, k), {axis: at(axis, 2 * c - 1, n)})

    def begin(net, j):
        for k in sorted({slot_of[j % n], slot_of[-j % n]}):
            for way, sign in enumerate((1, -1)):
                if goes(way, 0, k // half):
                    moving = piece(net, 0, k)
                    send(moving, moving, bsem(net, way, k),
                         {ring_axis[net]: at(ring_axis[net], sign, n)})

    seen = set()

    def need(net, way, s, h):
        if (net, way, s, h) in seen or not goes(way, s, h):
            return
        seen.add((net, way, s, h))
        sign = 1 if way == 0 else -1
        to = {ring_axis[net]: at(ring_axis[net], sign, n)}
        if s == 0:
            for k in range(h * half, (h + 1) * half):
                arrived(piece(net, -sign, k), bsem(net, way, k), to)
        else:
            arrived(sub(net, -sign * (s + 1), h), rsem(net, way, s, h), to)

    def ring(s, h):
        for net in range(2):
            for way, sign in enumerate((1, -1)):
                if goes(way, s, h):
                    need(net, way, s - 1, h)
                    moving = sub(net, -sign * s, h)
                    send(moving, moving, rsem(net, way, s, h),
                         {ring_axis[net]: at(ring_axis[net], sign, n)})

    for net in range(2):
        where = jnp.where(c == 0, position[net], position[2 + net])
        block = place[ring_axis[net]]
        weights[net, block, 0, c] = (heads[2 * c + net] - ortho[where, c]).astype(BF16)
        weights[net, block, 0, 1 - c] = (other_heads[net] - ortho[where, 1 - c]).astype(BF16)
        pass_on(net, 0)
        begin(net, 0)
    for j in range(1, half + 1):
        for net in range(2):
            axis = axes[net][0]
            for k in sorted({slot_of[j % n], slot_of[-j % n]}):
                arrived(piece(net, 0, k), fsem(net, k), {axis: at(axis, 1, n)})
            pass_on(net, j)
            begin(net, j)
        if j + 1 == half:
            ring(1, 0)

    for i in range(8):
        lanes = slice((i % 4) * HD, (i % 4 + 1) * HD)
        master[i // 4, :, lanes] = master[i // 4, :, lanes] - ortho[position[i], c]
    stores.append(pltpu.make_async_copy(master, new_master, store.at[1]))
    stores[1].start()

    def inverse_rms():
        mean = jnp.sum(squares[...], axis=1, keepdims=True) / d_model
        squares[...] = jnp.broadcast_to(lax.rsqrt(mean + rms_epsilon), squares.shape)

    def normalise(src, offset, k):
        tile = 32 if count % 32 == 0 else 16
        first = at(X, offset, 4) * blocks

        def body(i, _):
            r = pl.ds(pl.multiple_of(i * tile, tile), tile)
            inverse = squares[r]
            for j in range(blocks):
                v = src[r, j * HD : (j + 1) * HD].astype(F32)
                v = v * inverse * gain[pl.ds(first + j, 1), :]
                normed[first + j, c, r] = v.astype(BF16)
            return 0

        lax.fori_loop(0, count // tile, body, 0)
        made = normed.at[pl.ds(first, blocks), c]
        send(made, made, pair(3 + k), partner)

    def partner_normed(offset, k):
        first = at(X, offset, 4) * blocks
        arrived(normed.at[pl.ds(first, blocks), 1 - c], pair(3 + k), partner)

    def multiply(net, offset, fresh=False):
        block = at(ring_axis[net], offset, n)
        axis = axes[net][0]
        wide = []
        for o in order:
            across = at(axis, o, n)
            feature = block * n + across if net == 0 else across * n + block
            wide.append(normed[feature].reshape(2 * count, HD))
        product = dot(jnp.concatenate(wide, axis=1), weights[net, block].reshape(n * HD, HD))
        total[net] = product if fresh else total[net] + product

    def tokens_one():
        arrived(came_tokens.at[0, lower], tok(2), right)
        add_squares(came_tokens.at[0], False)

    def tokens_three():
        arrived(came_tokens.at[2, upper], tok(3), left)
        add_squares(came_tokens.at[2], False)

    def tokens_two():
        arrived(came_tokens.at[1, upper], tok(4), right)
        arrived(came_tokens.at[1, lower], tok(5), left)
        add_squares(came_tokens.at[1], False)
        inverse_rms()

    def own_block():
        for k, offset in enumerate((0, -1, 1, 2)):
            partner_normed(offset, k)
        for net in range(2):
            multiply(net, 0, True)

    def distance(k):
        for net in range(2):
            for h in range(2):
                for way in range(2):
                    need(net, way, k - 1, h)
            multiply(net, k)
            if k < half:
                multiply(net, -k)

    work = [
        [tokens_one],
        [tokens_three, tokens_two],
        [lambda: normalise(tokens, 0, 0), lambda: normalise(came_tokens.at[0], -1, 1)],
        [lambda: normalise(came_tokens.at[2], 1, 2), lambda: normalise(came_tokens.at[1], 2, 3)],
        [own_block, functools.partial(distance, 1)],
    ]
    work += [[functools.partial(distance, k)] for k in range(2, half + 1)]
    steps = [(s, h) for s in range(1, half) for h in range(2) if (s, h) != (1, 0)]
    for s, h in steps:
        for task in work.pop(0):
            task()
        ring(s, h)
    for tasks in work:
        for task in tasks:
            task()

    for net in range(2):
        kv_send[net] = total[net, pl.ds(pl.multiple_of((1 - c) * count, 16), count)].astype(BF16)
    send(kv_send, kv_blocks.at[pl.ds(2 * c, 2)], pair(7), partner)
    for net in range(2):
        kv_blocks[2 * c + net] = total[net, pl.ds(pl.multiple_of(c * count, 16), count)].astype(BF16)

    def store_columns(core, k):
        for net in range(2):
            block = 2 * core + net
            lanes = pl.ds(pl.multiple_of(block * HD, HD), HD)
            stores.append(
                pltpu.make_async_copy(kv_blocks.at[block], key_values.at[:, lanes], store.at[k + net])
            )
            stores[-1].start()

    store_columns(c, 2)
    finish_sends()
    arrived(kv_blocks.at[pl.ds(2 * (1 - c), 2)], pair(7), partner)
    store_columns(1 - c, 4)
    for copy in stores:
        copy.wait()


def hand_over(*refs):
    given, taken, done = refs[:3], refs[3:6], refs[6]
    copies = [pltpu.make_async_copy(a, b, done.at[k]) for k, (a, b) in enumerate(zip(given, taken))]
    for copy in copies:
        copy.start()
    for copy in copies:
        copy.wait()


def per_device(n, d_model, master, momentum, gradient, bucket_table, tokens, norm_gain):
    height = master.shape[1]
    count, width = tokens.shape
    blocks = width // HD
    rows = PACKED // n
    half = n // 2
    anywhere = pl.BlockSpec(memory_space=pl.ANY)
    dma = pltpu.SemaphoreType.DMA
    scratch = [
        pltpu.SMEM(bucket_table.shape, jnp.int32),
        *[pltpu.VMEM(master.shape, F32) for _ in range(3)],
        pltpu.VMEM(tokens.shape, BF16),
        pltpu.VMEM((4 * blocks, HD), F32),
        dma((6,)),
        dma((6,)),
        pltpu.VMEM((8, height, HD), F32),
        pltpu.VMEM((8, height, HD), F32),
        pltpu.VMEM((4, height, HD), F32),
        pltpu.VMEM((4, height, HD), F32),
        pltpu.VMEM((2, height, HD), F32),
        pltpu.VMEM((2, PACKED, HD), F32),
        pltpu.VMEM((2, n - 1, rows, HD), F32),
        pltpu.VMEM((2, rows, HD), F32),
        pltpu.VMEM((2, n - 1, rows, HD), F32),
        pltpu.VMEM((2, PACKED, HD), F32),
        pltpu.VMEM((8, 2, height, HD), F32),
        pltpu.VMEM((2, n, n, 2, height, HD), BF16),
        pltpu.VMEM((3, count, width), BF16),
        pltpu.VMEM((count, HD), F32),
        pltpu.VMEM((4 * blocks, 2, count, HD), BF16),
        pltpu.VMEM((2, 2 * count, HD), F32),
        pltpu.VMEM((2, count, HD), BF16),
        pltpu.VMEM((4, count, HD), BF16),
        dma((8,)),
        dma((8,)),
        dma((3, 2, n - 1)),
        dma((3, 2, n - 1)),
        dma((6,)),
        dma((6,)),
        dma((2, n)),
        dma((2, n)),
        dma((2, 2, n)),
        dma((2, 2, n)),
        dma((2, 2, half, 2)),
        dma((2, 2, half, 2)),
    ]
    outs = (
        jax.ShapeDtypeStruct(master.shape, F32),
        jax.ShapeDtypeStruct(master.shape, F32),
        jax.ShapeDtypeStruct((count, 4 * HD), BF16),
    )
    made = pl.pallas_call(
        functools.partial(kernel, n, d_model),
        out_shape=outs,
        in_specs=[anywhere] * 6,
        out_specs=(anywhere,) * 3,
        scratch_shapes=scratch,
        compiler_params=pltpu.CompilerParams(
            collective_id=0, has_side_effects=True, vmem_limit_bytes=60 * 1024 * 1024
        ),
    )(bucket_table, master, momentum, gradient, tokens, norm_gain.reshape(-1, HD))
    return pl.pallas_call(
        hand_over,
        out_shape=outs,
        in_specs=[anywhere] * 3,
        out_specs=(anywhere,) * 3,
        scratch_shapes=[dma((3,))],
    )(*made)


def solution(mesh):
    n = math.isqrt(mesh.shape["dp"] // 2)
    torus = Mesh(
        mesh.devices.reshape(n, n, 2, mesh.shape["tensor"]), ("dp_0", "dp_1", "dp_2", "tensor")
    )

    def whole(*args):
        return jax.shard_map(
            functools.partial(per_device, n, args[0].shape[1]),
            mesh=torus,
            in_specs=(
                P(None, DP, "tensor"),
                P(None, DP, "tensor"),
                P(None, DP, "tensor"),
                P("tensor", None),
                P(DP, "tensor"),
                P(),
            ),
            out_specs=(P(None, DP, "tensor"), P(None, DP, "tensor"), P(DP, "tensor")),
            check_vma=False,
        )(*args)

    return whole
```

```python
import functools
import math

import jax
import jax.numpy as jnp
from jax import lax
from jax.experimental import pallas as pl
from jax.experimental.pallas import tpu as pltpu
from jax.sharding import Mesh
from jax.sharding import PartitionSpec as P

HD = 128
NS_ITERS = 3
DP = ("dp_0", "dp_1", "dp_2")

beta_momentum = 0.95
learn_rate = 0.05
first_coeff = 3.4445
cube_coeff = -4.775
fifth_coeff = 2.0315
frob_epsilon = 1e-07
rms_epsilon = 1e-05

F32 = jnp.float32
BF16 = jnp.bfloat16
Y, Z, C, X = "dp_1", "dp_0", "dp_2", "tensor"
PACKED = 2 * HD + 64


def near_first(n):
    offsets = [0]
    for k in range(1, n // 2):
        offsets += [k, -k]
    return [*offsets, n // 2]


def split(a):
    high = a.astype(BF16)
    return high, (a - high.astype(F32)).astype(BF16)


def dot(a, b):
    return jnp.dot(a, b, preferred_element_type=F32)


def dot3(a, b):
    return dot(a[0], b[0]) + (dot(a[0], b[1]) + dot(a[1], b[0]))


def kernel(n, d_model, table_in, master_in, momentum_in, gradient_in, tokens_in, gain_in, new_master,
           new_momentum, key_values, table, master, momentum, gradient, tokens, gain, load, update,
           stacked, other_rows, heads, other_heads, packed, came1, part, came2, gram, ortho, weights,
           came_tokens, squares, normed, total, kv_send, kv_blocks, pair_send, pair_recv, gram_send,
           gram_recv, token_send, token_recv, first_send, first_recv, ring_send,
           ring_recv):
    half = n // 2
    rows = PACKED // n
    count = tokens.shape[0]
    blocks = tokens.shape[1] // HD
    height = master.shape[1]
    z, y, c, x = (lax.axis_index(a) for a in (Z, Y, C, X))
    axes = ((Y, Z), (Z, Y))
    place = {Y: y, Z: z}
    pending = []

    def at(axis, offset, size):
        here = {Y: y, Z: z, X: x}[axis]
        return lax.rem(here + (offset + size), size)

    def send(src, dst, sems, to):
        copy = pltpu.make_async_remote_copy(
            src_ref=src, dst_ref=dst, send_sem=sems[0], recv_sem=sems[1],
            device_id=to, device_id_type=pl.DeviceIdType.MESH,
        )
        copy.start()
        pending.append(copy)

    def arrived(ref, sems, to):
        pltpu.make_async_remote_copy(
            src_ref=ref, dst_ref=ref, send_sem=sems[0], recv_sem=sems[1],
            device_id=to, device_id_type=pl.DeviceIdType.MESH,
        ).wait_recv()

    def finish_sends():
        while pending:
            pending.pop(0).wait_send()

    partner = {C: 1 - c}

    barrier = pltpu.get_barrier_semaphore()
    greeted = [partner, {X: at(X, 1, 4)}, {X: at(X, -1, 4)}]
    for axis in (Y, Z):
        greeted += [{axis: at(axis, d, n)} for d in range(1, n)]
    for device in greeted:
        pl.semaphore_signal(barrier, inc=1, device_id=device, device_id_type=pl.DeviceIdType.MESH)

    loads = [
        pltpu.make_async_copy(src, dst, load.at[k])
        for k, (src, dst) in enumerate((
            (table_in, table), (gradient_in, gradient), (momentum_in, momentum),
            (master_in, master), (tokens_in, tokens), (gain_in, gain),
        ))
    ]
    for copy in loads:
        copy.start()
    loads[0].wait()

    bucket = [table[0, i] for i in range(8)]
    position = []
    for i in range(8):
        earlier = jnp.int32(0)
        for j in range(i):
            earlier += jnp.where(bucket[j] == bucket[i], 1, 0)
        position.append(2 * bucket[i] + earlier)
    held = []
    for s in range(8):
        which = jnp.int32(0)
        for i in range(8):
            which += jnp.where(position[i] == s, i, 0)
        held.append(which)

    for copy in loads[1:4]:
        copy.wait()
    for layer in range(2):
        for slot in range(4):
            lanes = slice(slot * HD, (slot + 1) * HD)
            g = gradient[layer, :, lanes]
            m = beta_momentum * momentum[layer, :, lanes] + g
            new_momentum[layer, :, lanes] = m
            update[layer * 4 + slot] = g + beta_momentum * m
            if layer == 0:
                heads[slot] = master[0, :, lanes]
    for s in range(8):
        stacked[s] = update[held[s]]

    pl.semaphore_wait(barrier, len(greeted))

    def pair(k):
        return pair_send.at[k], pair_recv.at[k]

    send(stacked.at[pl.ds(4 * (1 - c), 4)], other_rows, pair(0), partner)
    send(heads.at[pl.ds(2 * (1 - c), 2)], other_heads, pair(1), partner)

    right, left = {X: at(X, 1, 4)}, {X: at(X, -1, 4)}
    upper, lower = pl.ds(0, count // 2), pl.ds(count // 2, count // 2)

    for copy in loads[4:]:
        copy.wait()

    def tok(k):
        return token_send.at[k], token_recv.at[k]

    send(tokens.at[upper], came_tokens.at[0, upper], tok(0), right)
    send(tokens.at[lower], came_tokens.at[2, lower], tok(1), left)
    send(tokens.at[lower], came_tokens.at[0, lower], tok(2), right)
    send(tokens.at[upper], came_tokens.at[2, upper], tok(3), left)

    arrived(other_rows, pair(0), partner)

    def chip_rows(b):
        own = jnp.concatenate([stacked[4 * c + 2 * b], stacked[4 * c + 2 * b + 1]], axis=1)
        other = jnp.concatenate([other_rows[2 * b], other_rows[2 * b + 1]], axis=1)
        return jnp.concatenate([own, other], axis=0)

    def lines(ref, net, chunk):
        return ref.at[net, pl.ds(pl.multiple_of(chunk * rows, 8), rows)]

    far_first = [o % n for o in reversed(near_first(n)[1:])]

    def gsem(stage, net, d):
        return gram_send.at[stage, net, d - 1], gram_recv.at[stage, net, d - 1]

    r_id = lax.broadcasted_iota(jnp.int32, (HD, HD), 0)
    c_id = lax.broadcasted_iota(jnp.int32, (HD, HD), 1)
    for net in range(2):
        s = chip_rows(net)
        g = dot3(split(s.T), split(s))
        second = g[HD:, HD:]
        packed[net, 0:HD] = jnp.where(r_id <= c_id, g[:HD, :HD], second)
        packed[net, HD : 2 * HD] = g[:HD, HD:]
        diagonal = jnp.sum(jnp.where(r_id == c_id, second, 0.0), axis=0, keepdims=True)
        packed[net, 2 * HD :] = jnp.broadcast_to(diagonal, (PACKED - 2 * HD, HD))
        axis = axes[net][0]
        for d in far_first:
            to = at(axis, d, n)
            send(lines(packed, net, to), came1.at[net, d - 1], gsem(0, net, d), {axis: to})

    def add_squares(src, fresh):
        tile = 32 if count % 32 == 0 else 16

        def body(i, _):
            r = pl.ds(pl.multiple_of(i * tile, tile), tile)
            t = jnp.zeros((tile, HD), F32) if fresh else squares[r]
            for j in range(blocks):
                v = src[r, j * HD : (j + 1) * HD].astype(F32)
                t = t + v * v
            squares[r] = t
            return 0

        lax.fori_loop(0, count // tile, body, 0)

    add_squares(tokens, True)

    for net in range(2):
        axis, other = axes[net]
        for d in range(1, n):
            arrived(came1.at[net, d - 1], gsem(0, net, d), {axis: at(axis, d, n)})
        s = packed[net, pl.ds(pl.multiple_of(place[axis] * rows, 8), rows)]
        for d in range(1, n):
            s = s + came1[net, d - 1]
        part[net] = s
        for d in far_first:
            send(part.at[net], came2.at[net, d - 1], gsem(1, net, d), {other: at(other, d, n)})
    for net in range(2):
        axis, other = axes[net]
        for d in range(1, n):
            arrived(came2.at[net, d - 1], gsem(1, net, d), {other: at(other, d, n)})
        s = part[net]
        for d in range(1, n):
            s = s + came2[net, d - 1]
        gram[net, pl.ds(pl.multiple_of(place[axis] * rows, 8), rows)] = s
        own = lines(gram, net, place[axis])
        for d in far_first:
            send(own, own, gsem(2, net, d), {axis: at(axis, d, n)})

    arrived(came_tokens.at[0, upper], tok(0), right)
    send(came_tokens.at[0, upper], came_tokens.at[1, upper], tok(4), right)
    arrived(came_tokens.at[2, lower], tok(1), left)
    send(came_tokens.at[2, lower], came_tokens.at[1, lower], tok(5), left)

    for net in range(2):
        axis = axes[net][0]
        for d in range(1, n):
            arrived(lines(gram, net, at(axis, -d, n)), gsem(2, net, d), {axis: at(axis, d, n)})

    eye = jnp.where(
        lax.broadcasted_iota(jnp.int32, (2 * HD, 2 * HD), 0)
        == lax.broadcasted_iota(jnp.int32, (2 * HD, 2 * HD), 1), 1.0, 0.0
    ).astype(F32)
    grams, scales, products = [], [], [None, None]
    for net in range(2):
        both, corner = gram[net, 0:HD], gram[net, HD : 2 * HD]
        turned = both.T
        one = jnp.where(r_id <= c_id, both, turned)
        two = jnp.where(r_id > c_id, both, jnp.where(r_id < c_id, turned, gram[net, 2 * HD : 2 * HD + 1]))
        top = jnp.concatenate([one, corner], axis=1)
        bottom = jnp.concatenate([corner.T, two], axis=1)
        g = jnp.concatenate([top, bottom], axis=0)
        trace = jnp.sum(jnp.sum(g * eye, axis=1, keepdims=True), axis=0, keepdims=True)
        scale = 1.0 / (jnp.sqrt(trace) + frob_epsilon)
        grams.append(g * (scale * scale))
        scales.append(scale)
    for iteration in range(NS_ITERS):
        gs = [split(g) for g in grams]
        squared = [dot3(g, g) for g in gs]
        factor = [
            first_coeff * eye + (cube_coeff * g + fifth_coeff * q) for g, q in zip(grams, squared)
        ]
        fs = [split(f) for f in factor]
        if iteration == 0:
            products = factor
        else:
            products = [dot3(split(p), f) for p, f in zip(products, fs)]
        if iteration + 1 < NS_ITERS:
            half_way = [dot3(f, g) for f, g in zip(fs, gs)]
            grams = [dot3(split(h), f) for h, f in zip(half_way, fs)]

    step = learn_rate * math.sqrt(max(1.0, d_model / (2.0 * HD)))
    for net in range(2):
        moved = dot3(split(chip_rows(net)), split(products[net] * (scales[net] * step)))
        for h in range(2):
            lanes = slice(h * HD, (h + 1) * HD)
            ortho[4 * c + 2 * net + h, c] = moved[:height, lanes]
            ortho[4 * c + 2 * net + h, 1 - c] = moved[height:, lanes]
    mine = ortho.at[pl.ds(4 * c, 4)]
    send(mine, mine, pair(2), partner)
    arrived(other_heads, pair(1), partner)
    arrived(ortho.at[pl.ds(4 * (1 - c), 4)], pair(2), partner)

    order = near_first(n)
    slot_of = {o % n: k for k, o in enumerate(order)}
    ring_axis = (Z, Y)

    near = n // 4
    groups = ((0, 1), (1, 2 * near + 1), (2 * near + 1, n))

    def rsem(net, way, s, g):
        return ring_send.at[net, way, s, g], ring_recv.at[net, way, s, g]

    def fsem(net, k):
        return first_send.at[net, k], first_recv.at[net, k]

    def sub(net, offset, g):
        low, high = groups[g]
        return weights.at[net, at(ring_axis[net], offset, n), pl.ds(low, high - low)]

    def piece(net, k):
        return weights.at[net, place[ring_axis[net]], k]

    def give(net, target, source, to):
        k = slot_of[target % n]
        send(piece(net, source), piece(net, k), fsem(net, k), {axes[net][0]: at(axes[net][0], to, n)})

    def give_near(net):
        for t in range(1, near + 1):
            give(net, t, 0, -t)
            give(net, -t, 0, t)

    def give_far(net):
        ahead, behind = slot_of[near % n], slot_of[-near % n]
        for t in range(near + 1, half):
            give(net, t, ahead, near - t)
            give(net, -t, behind, t - near)
        give(net, half, jnp.where(c == 0, ahead, behind), (2 * c - 1) * (half - near))

    def first_came(net, g):
        for k in range(*groups[g]):
            arrived(piece(net, k), fsem(net, k), {axes[net][0]: at(axes[net][0], 1, n)})

    def goes(way, s, g):
        low, high = groups[g]
        return low < high and (s + 1 < half or way == g % 2)

    seen = set()

    def need(net, way, s, g):
        if (net, way, s, g) in seen or not goes(way, s, g):
            return
        seen.add((net, way, s, g))
        sign = 1 if way == 0 else -1
        arrived(sub(net, -sign * (s + 1), g), rsem(net, way, s, g),
                {ring_axis[net]: at(ring_axis[net], sign, n)})

    def ring(s, g):
        if s >= half:
            return
        for net in range(2):
            for way, sign in enumerate((1, -1)):
                if goes(way, s, g):
                    if s > 0:
                        need(net, way, s - 1, g)
                    moving = sub(net, -sign * s, g)
                    send(moving, moving, rsem(net, way, s, g),
                         {ring_axis[net]: at(ring_axis[net], sign, n)})

    for net in range(2):
        where = jnp.where(c == 0, position[net], position[2 + net])
        block = place[ring_axis[net]]
        weights[net, block, 0, c] = (heads[2 * c + net] - ortho[where, c]).astype(BF16)
        weights[net, block, 0, 1 - c] = (other_heads[net] - ortho[where, 1 - c]).astype(BF16)
        give_near(net)
    ring(0, 0)
    for net in range(2):
        first_came(net, 1)
        give_far(net)
    ring(0, 1)

    for i in range(8):
        lanes = slice((i % 4) * HD, (i % 4 + 1) * HD)
        new_master[i // 4, :, lanes] = master[i // 4, :, lanes] - ortho[position[i], c]
    ring(1, 0)
    for net in range(2):
        first_came(net, 2)
    ring(0, 2)
    ring(2, 0)

    def inverse_rms():
        mean = jnp.sum(squares[...], axis=1, keepdims=True) / d_model
        squares[...] = jnp.broadcast_to(lax.rsqrt(mean + rms_epsilon), squares.shape)

    def normalise(src, offset, k):
        tile = 32 if count % 32 == 0 else 16
        first = at(X, offset, 4) * blocks

        def body(i, _):
            r = pl.ds(pl.multiple_of(i * tile, tile), tile)
            inverse = squares[r]
            for j in range(blocks):
                v = src[r, j * HD : (j + 1) * HD].astype(F32)
                v = v * inverse * gain[pl.ds(first + j, 1), :]
                normed[first + j, c, r] = v.astype(BF16)
            return 0

        lax.fori_loop(0, count // tile, body, 0)
        made = normed.at[pl.ds(first, blocks), c]
        send(made, made, pair(3 + k), partner)

    def partner_normed(offset, k):
        first = at(X, offset, 4) * blocks
        arrived(normed.at[pl.ds(first, blocks), 1 - c], pair(3 + k), partner)

    def multiply(net, offset, low=0, high=n, fresh=False):
        block = at(ring_axis[net], offset, n)
        axis = axes[net][0]
        wide = []
        for o in order[low:high]:
            across = at(axis, o, n)
            feature = block * n + across if net == 0 else across * n + block
            wide.append(normed[feature].reshape(2 * count, HD))
        rhs = weights[net, block, low:high].reshape((high - low) * HD, HD)
        product = dot(jnp.concatenate(wide, axis=1), rhs)
        total[net] = product if fresh else total[net] + product

    def tokens_one():
        arrived(came_tokens.at[0, lower], tok(2), right)
        add_squares(came_tokens.at[0], False)

    def tokens_three():
        arrived(came_tokens.at[2, upper], tok(3), left)
        add_squares(came_tokens.at[2], False)

    def tokens_two():
        arrived(came_tokens.at[1, upper], tok(4), right)
        arrived(came_tokens.at[1, lower], tok(5), left)
        add_squares(came_tokens.at[1], False)
        inverse_rms()

    def own_block():
        for k, offset in enumerate((0, -1, 1, 2)):
            partner_normed(offset, k)
        for net in range(2):
            multiply(net, 0, fresh=True)

    def distance(k):
        for net in range(2):
            for g in range(3):
                for way in range(2):
                    need(net, way, k - 1, g)
            multiply(net, k)
            multiply(net, -k)

    work = [
        (lambda: ring(1, 1), tokens_one),
        (lambda: ring(3, 0), tokens_three, tokens_two),
        (lambda: ring(1, 2), lambda: normalise(tokens, 0, 0), lambda: normalise(came_tokens.at[0], -1, 1)),
        (lambda: ring(2, 1), lambda: normalise(came_tokens.at[2], 1, 2),
         lambda: normalise(came_tokens.at[1], 2, 3)),
        (lambda: ring(2, 2), own_block),
        (lambda: ring(3, 1), lambda: ring(3, 2)),
    ]
    for tasks in work:
        for task in tasks:
            task()
    for k in range(1, half):
        distance(k)

    for net in range(2):
        for g in (0, 1, 2):
            for way in range(2):
                need(net, way, half - 1, g)
        multiply(net, half)
        kv_send[net] = total[net, pl.ds(pl.multiple_of((1 - c) * count, 16), count)].astype(BF16)
        send(kv_send.at[net], kv_blocks.at[2 * c + net], pair(7 + net), partner)
    for net in range(2):
        kv_blocks[2 * c + net] = total[net, pl.ds(pl.multiple_of(c * count, 16), count)].astype(BF16)
    finish_sends()
    for net in range(2):
        arrived(kv_blocks.at[2 * (1 - c) + net], pair(7 + net), partner)
    for k in range(4):
        key_values[:, k * HD : (k + 1) * HD] = kv_blocks[k]


def hand_over(*refs):
    given, taken, done = refs[:3], refs[3:6], refs[6]
    copies = [pltpu.make_async_copy(a, b, done.at[k]) for k, (a, b) in enumerate(zip(given, taken))]
    for copy in copies:
        copy.start()
    for copy in copies:
        copy.wait()


def per_device(n, d_model, master, momentum, gradient, bucket_table, tokens, norm_gain):
    height = master.shape[1]
    count, width = tokens.shape
    blocks = width // HD
    rows = PACKED // n
    half = n // 2
    hbm, anywhere, vmem = (pl.BlockSpec(memory_space=m) for m in (pltpu.HBM, pl.ANY, pltpu.VMEM))
    dma = pltpu.SemaphoreType.DMA
    scratch = [
        pltpu.SMEM(bucket_table.shape, jnp.int32),
        *[pltpu.VMEM(master.shape, F32) for _ in range(3)],
        pltpu.VMEM(tokens.shape, BF16),
        pltpu.VMEM((4 * blocks, HD), F32),
        dma((6,)),
        pltpu.VMEM((8, height, HD), F32),
        pltpu.VMEM((8, height, HD), F32),
        pltpu.VMEM((4, height, HD), F32),
        pltpu.VMEM((4, height, HD), F32),
        pltpu.VMEM((2, height, HD), F32),
        pltpu.VMEM((2, PACKED, HD), F32),
        pltpu.VMEM((2, n - 1, rows, HD), F32),
        pltpu.VMEM((2, rows, HD), F32),
        pltpu.VMEM((2, n - 1, rows, HD), F32),
        pltpu.VMEM((2, PACKED, HD), F32),
        pltpu.VMEM((8, 2, height, HD), F32),
        pltpu.VMEM((2, n, n, 2, height, HD), BF16),
        pltpu.VMEM((3, count, width), BF16),
        pltpu.VMEM((count, HD), F32),
        pltpu.VMEM((4 * blocks, 2, count, HD), BF16),
        pltpu.VMEM((2, 2 * count, HD), F32),
        pltpu.VMEM((2, count, HD), BF16),
        pltpu.VMEM((4, count, HD), BF16),
        dma((9,)),
        dma((9,)),
        dma((3, 2, n - 1)),
        dma((3, 2, n - 1)),
        dma((6,)),
        dma((6,)),
        dma((2, n)),
        dma((2, n)),
        dma((2, 2, half, 3)),
        dma((2, 2, half, 3)),
    ]
    outs = (
        jax.ShapeDtypeStruct(master.shape, F32),
        jax.ShapeDtypeStruct(master.shape, F32),
        jax.ShapeDtypeStruct((count, 4 * HD), BF16),
    )
    made = pl.pallas_call(
        functools.partial(kernel, n, d_model),
        out_shape=outs,
        in_specs=[hbm] * 6,
        out_specs=(vmem,) * 3,
        scratch_shapes=scratch,
        compiler_params=pltpu.CompilerParams(
            collective_id=0, has_side_effects=True, vmem_limit_bytes=48 * 1024 * 1024
        ),
    )(*(
        pltpu.with_memory_space_constraint(a, pltpu.HBM)
        for a in (bucket_table, master, momentum, gradient, tokens, norm_gain.reshape(-1, HD))
    ))
    return pl.pallas_call(
        hand_over,
        out_shape=outs,
        in_specs=[vmem] * 3,
        out_specs=(hbm,) * 3,
        scratch_shapes=[dma((3,))],
        compiler_params=pltpu.CompilerParams(vmem_limit_bytes=4 * 1024 * 1024),
    )(*made)


def solution(mesh):
    n = math.isqrt(mesh.shape["dp"] // 2)
    torus = Mesh(
        mesh.devices.reshape(n, n, 2, mesh.shape["tensor"]), ("dp_0", "dp_1", "dp_2", "tensor")
    )

    def whole(*args):
        return jax.shard_map(
            functools.partial(per_device, n, args[0].shape[1]),
            mesh=torus,
            in_specs=(
                P(None, DP, "tensor"),
                P(None, DP, "tensor"),
                P(None, DP, "tensor"),
                P("tensor", None),
                P(DP, "tensor"),
                P(),
            ),
            out_specs=(P(None, DP, "tensor"), P(None, DP, "tensor"), P(DP, "tensor")),
            check_vma=False,
        )(*args)

    return whole
```

```python
import functools
import math

import jax
import jax.numpy as jnp
from jax import lax
from jax.experimental import pallas as pl
from jax.experimental.pallas import tpu as pltpu
from jax.sharding import Mesh
from jax.sharding import PartitionSpec as P

HD = 128
NS_ITERS = 3
DP = ("dp_0", "dp_1", "dp_2")

beta_momentum = 0.95
learn_rate = 0.05
first_coeff = 3.4445
cube_coeff = -4.775
fifth_coeff = 2.0315
frob_epsilon = 1e-07
rms_epsilon = 1e-05

F32 = jnp.float32
BF16 = jnp.bfloat16
Y, Z, C, X = "dp_1", "dp_0", "dp_2", "tensor"
PACKED = 2 * HD + 64


def near_first(n):
    offsets = [0]
    for k in range(1, n // 2):
        offsets += [k, -k]
    return [*offsets, n // 2]


def split(a):
    high = a.astype(BF16)
    return high, (a - high.astype(F32)).astype(BF16)


def dot(a, b):
    return jnp.dot(a, b, preferred_element_type=F32)


def dot3(a, b):
    return dot(a[0], b[0]) + (dot(a[0], b[1]) + dot(a[1], b[0]))


def kernel(n, d_model, table_in, master_in, momentum_in, gradient_in, tokens_in, gain_in, new_master,
           new_momentum, key_values, table, master, momentum, gradient, tokens, gain, load, update,
           stacked, other_rows, heads, other_heads, packed, came1, part, came2, gram, ortho, weights,
           came_tokens, squares, normed, total, kv_send, kv_blocks, pair_send, pair_recv, gram_send,
           gram_recv, token_send, token_recv, first_send, first_recv, ring_send,
           ring_recv):
    half = n // 2
    rows = PACKED // n
    count = tokens.shape[0]
    blocks = tokens.shape[1] // HD
    height = master.shape[1]
    z, y, c, x = (lax.axis_index(a) for a in (Z, Y, C, X))
    axes = ((Y, Z), (Z, Y))
    place = {Y: y, Z: z}
    pending = []

    def at(axis, offset, size):
        here = {Y: y, Z: z, X: x}[axis]
        return lax.rem(here + (offset + size), size)

    def send(src, dst, sems, to):
        copy = pltpu.make_async_remote_copy(
            src_ref=src, dst_ref=dst, send_sem=sems[0], recv_sem=sems[1],
            device_id=to, device_id_type=pl.DeviceIdType.MESH,
        )
        copy.start()
        pending.append(copy)

    def arrived(ref, sems, to):
        pltpu.make_async_remote_copy(
            src_ref=ref, dst_ref=ref, send_sem=sems[0], recv_sem=sems[1],
            device_id=to, device_id_type=pl.DeviceIdType.MESH,
        ).wait_recv()

    def settle(keep):
        while len(pending) > keep:
            pending.pop(0).wait_send()

    partner = {C: 1 - c}

    barrier = pltpu.get_barrier_semaphore()
    greeted = [partner, {X: at(X, 1, 4)}, {X: at(X, -1, 4)}]
    for axis in (Y, Z):
        greeted += [{axis: at(axis, d, n)} for d in range(1, n)]
    for device in greeted:
        pl.semaphore_signal(barrier, inc=1, device_id=device, device_id_type=pl.DeviceIdType.MESH)

    loads = [
        pltpu.make_async_copy(src, dst, load.at[k])
        for k, (src, dst) in enumerate((
            (table_in, table), (gradient_in, gradient), (momentum_in, momentum),
            (master_in, master), (tokens_in, tokens), (gain_in, gain),
        ))
    ]
    for copy in loads:
        copy.start()
    loads[0].wait()

    bucket = [table[0, i] for i in range(8)]
    position = []
    for i in range(8):
        earlier = jnp.int32(0)
        for j in range(i):
            earlier += jnp.where(bucket[j] == bucket[i], 1, 0)
        position.append(2 * bucket[i] + earlier)
    held = []
    for s in range(8):
        which = jnp.int32(0)
        for i in range(8):
            which += jnp.where(position[i] == s, i, 0)
        held.append(which)

    for copy in loads[1:4]:
        copy.wait()
    for layer in range(2):
        for slot in range(4):
            lanes = slice(slot * HD, (slot + 1) * HD)
            g = gradient[layer, :, lanes]
            m = beta_momentum * momentum[layer, :, lanes] + g
            new_momentum[layer, :, lanes] = m
            update[layer * 4 + slot] = g + beta_momentum * m
            if layer == 0:
                heads[slot] = master[0, :, lanes]
    for s in range(8):
        stacked[s] = update[held[s]]

    pl.semaphore_wait(barrier, len(greeted))

    def pair(k):
        return pair_send.at[k], pair_recv.at[k]

    send(stacked.at[pl.ds(4 * (1 - c), 4)], other_rows, pair(0), partner)
    send(heads.at[pl.ds(2 * (1 - c), 2)], other_heads, pair(1), partner)

    right, left = {X: at(X, 1, 4)}, {X: at(X, -1, 4)}
    upper, lower = pl.ds(0, count // 2), pl.ds(count // 2, count // 2)

    for copy in loads[4:]:
        copy.wait()

    def tok(k):
        return token_send.at[k], token_recv.at[k]

    send(tokens.at[upper], came_tokens.at[0, upper], tok(0), right)
    send(tokens.at[lower], came_tokens.at[2, lower], tok(1), left)
    send(tokens.at[lower], came_tokens.at[0, lower], tok(2), right)
    send(tokens.at[upper], came_tokens.at[2, upper], tok(3), left)

    arrived(other_rows, pair(0), partner)

    def chip_rows(b):
        own = jnp.concatenate([stacked[4 * c + 2 * b], stacked[4 * c + 2 * b + 1]], axis=1)
        other = jnp.concatenate([other_rows[2 * b], other_rows[2 * b + 1]], axis=1)
        return jnp.concatenate([own, other], axis=0)

    parts = ((0, 16), (16, rows))

    def lines(ref, net, chunk, p):
        low, high = parts[p]
        return ref.at[net, pl.ds(pl.multiple_of(chunk * rows + low, 8), high - low)]

    def some(ref, net, d, p):
        low, high = parts[p]
        return ref.at[net, d - 1, pl.ds(low, high - low)]

    far_first = [o % n for o in reversed(near_first(n)[1:])]

    def gsem(stage, net, p, d):
        return gram_send.at[stage, net, p, d - 1], gram_recv.at[stage, net, p, d - 1]

    r_id = lax.broadcasted_iota(jnp.int32, (HD, HD), 0)
    c_id = lax.broadcasted_iota(jnp.int32, (HD, HD), 1)
    for net in range(2):
        s = chip_rows(net)
        g = dot3(split(s.T), split(s))
        second = g[HD:, HD:]
        packed[net, 0:HD] = jnp.where(r_id <= c_id, g[:HD, :HD], second)
        packed[net, HD : 2 * HD] = g[:HD, HD:]
        diagonal = jnp.sum(jnp.where(r_id == c_id, second, 0.0), axis=0, keepdims=True)
        packed[net, 2 * HD :] = jnp.broadcast_to(diagonal, (PACKED - 2 * HD, HD))
    for p in range(2):
        for net in range(2):
            axis = axes[net][0]
            for d in far_first:
                to = at(axis, d, n)
                send(lines(packed, net, to, p), some(came1, net, d, p), gsem(0, net, p, d), {axis: to})

    def add_squares(src, fresh):
        tile = 32 if count % 32 == 0 else 16

        def body(i, _):
            r = pl.ds(pl.multiple_of(i * tile, tile), tile)
            t = jnp.zeros((tile, HD), F32) if fresh else squares[r]
            for j in range(blocks):
                v = src[r, j * HD : (j + 1) * HD].astype(F32)
                t = t + v * v
            squares[r] = t
            return 0

        lax.fori_loop(0, count // tile, body, 0)

    add_squares(tokens, True)

    for p, (low, high) in enumerate(parts):
        for net in range(2):
            axis, other = axes[net]
            for d in range(1, n):
                arrived(some(came1, net, d, p), gsem(0, net, p, d), {axis: at(axis, d, n)})
            t = lines(packed, net, place[axis], p)[...]
            for d in range(1, n):
                t = t + came1[net, d - 1, low:high]
            part[net, low:high] = t
            for d in far_first:
                send(part.at[net, pl.ds(low, high - low)], some(came2, net, d, p), gsem(1, net, p, d),
                     {other: at(other, d, n)})
    for p, (low, high) in enumerate(parts):
        for net in range(2):
            axis, other = axes[net]
            for d in range(1, n):
                arrived(some(came2, net, d, p), gsem(1, net, p, d), {other: at(other, d, n)})
            t = part[net, low:high]
            for d in range(1, n):
                t = t + came2[net, d - 1, low:high]
            own = lines(gram, net, place[axis], p)
            own[...] = t
            for d in far_first:
                send(own, own, gsem(2, net, p, d), {axis: at(axis, d, n)})

    arrived(came_tokens.at[0, upper], tok(0), right)
    send(came_tokens.at[0, upper], came_tokens.at[1, upper], tok(4), right)
    arrived(came_tokens.at[2, lower], tok(1), left)
    send(came_tokens.at[2, lower], came_tokens.at[1, lower], tok(5), left)

    for net in range(2):
        axis = axes[net][0]
        for p in range(2):
            for d in range(1, n):
                arrived(lines(gram, net, at(axis, -d, n), p), gsem(2, net, p, d), {axis: at(axis, d, n)})

    eye = jnp.where(
        lax.broadcasted_iota(jnp.int32, (2 * HD, 2 * HD), 0)
        == lax.broadcasted_iota(jnp.int32, (2 * HD, 2 * HD), 1), 1.0, 0.0
    ).astype(F32)
    grams, scales, products = [], [], [None, None]
    for net in range(2):
        both, corner = gram[net, 0:HD], gram[net, HD : 2 * HD]
        turned = both.T
        one = jnp.where(r_id <= c_id, both, turned)
        two = jnp.where(r_id > c_id, both, jnp.where(r_id < c_id, turned, gram[net, 2 * HD : 2 * HD + 1]))
        top = jnp.concatenate([one, corner], axis=1)
        bottom = jnp.concatenate([corner.T, two], axis=1)
        g = jnp.concatenate([top, bottom], axis=0)
        trace = jnp.sum(jnp.sum(g * eye, axis=1, keepdims=True), axis=0, keepdims=True)
        scale = 1.0 / (jnp.sqrt(trace) + frob_epsilon)
        grams.append(g * (scale * scale))
        scales.append(scale)
    for iteration in range(NS_ITERS):
        gs = [split(g) for g in grams]
        squared = [dot3(g, g) for g in gs]
        factor = [
            first_coeff * eye + (cube_coeff * g + fifth_coeff * q) for g, q in zip(grams, squared)
        ]
        fs = [split(f) for f in factor]
        if iteration == 0:
            products = factor
        else:
            products = [dot3(split(p), f) for p, f in zip(products, fs)]
        if iteration + 1 < NS_ITERS:
            half_way = [dot3(f, g) for f, g in zip(fs, gs)]
            grams = [dot3(split(h), f) for h, f in zip(half_way, fs)]

    step = learn_rate * math.sqrt(max(1.0, d_model / (2.0 * HD)))
    for net in range(2):
        moved = dot3(split(chip_rows(net)), split(products[net] * (scales[net] * step)))
        for h in range(2):
            lanes = slice(h * HD, (h + 1) * HD)
            ortho[4 * c + 2 * net + h, c] = moved[:height, lanes]
            ortho[4 * c + 2 * net + h, 1 - c] = moved[height:, lanes]
        mine = ortho.at[pl.ds(4 * c + 2 * net, 2)]
        send(mine, mine, pair((2, 9)[net]), partner)
    arrived(other_heads, pair(1), partner)
    for net in range(2):
        arrived(ortho.at[pl.ds(4 * (1 - c) + 2 * net, 2)], pair((2, 9)[net]), partner)

    order = near_first(n)
    slot_of = {o % n: k for k, o in enumerate(order)}
    ring_axis = (Z, Y)

    near = n // 4
    groups = ((0, 1), (1, 2 * near + 1), (2 * near + 1, n))

    def rsem(net, way, s, g):
        return ring_send.at[net, way, s, g], ring_recv.at[net, way, s, g]

    def fsem(net, k):
        return first_send.at[net, k], first_recv.at[net, k]

    def sub(net, offset, g):
        low, high = groups[g]
        return weights.at[net, at(ring_axis[net], offset, n), pl.ds(low, high - low)]

    def piece(net, k):
        return weights.at[net, place[ring_axis[net]], k]

    def give(net, target, source, to):
        k = slot_of[target % n]
        send(piece(net, source), piece(net, k), fsem(net, k), {axes[net][0]: at(axes[net][0], to, n)})

    def give_near(net):
        for t in range(1, near + 1):
            give(net, t, 0, -t)
            give(net, -t, 0, t)

    def give_far(net):
        ahead, behind = slot_of[near % n], slot_of[-near % n]
        for t in range(near + 1, half):
            give(net, t, ahead, near - t)
            give(net, -t, behind, t - near)
        give(net, half, jnp.where(c == 0, ahead, behind), (2 * c - 1) * (half - near))

    def first_came(net, g):
        for k in range(*groups[g]):
            arrived(piece(net, k), fsem(net, k), {axes[net][0]: at(axes[net][0], 1, n)})

    def goes(way, s, g):
        low, high = groups[g]
        return low < high and (s + 1 < half or way == g % 2)

    seen = set()

    def need(net, way, s, g):
        if (net, way, s, g) in seen or not goes(way, s, g):
            return
        seen.add((net, way, s, g))
        sign = 1 if way == 0 else -1
        arrived(sub(net, -sign * (s + 1), g), rsem(net, way, s, g),
                {ring_axis[net]: at(ring_axis[net], sign, n)})

    def ring(s, g):
        if s >= half:
            return
        for net in range(2):
            for way, sign in enumerate((1, -1)):
                if goes(way, s, g):
                    if s > 0:
                        need(net, way, s - 1, g)
                    moving = sub(net, -sign * s, g)
                    send(moving, moving, rsem(net, way, s, g),
                         {ring_axis[net]: at(ring_axis[net], sign, n)})

    for net in range(2):
        where = jnp.where(c == 0, position[net], position[2 + net])
        block = place[ring_axis[net]]
        weights[net, block, 0, c] = (heads[2 * c + net] - ortho[where, c]).astype(BF16)
        weights[net, block, 0, 1 - c] = (other_heads[net] - ortho[where, 1 - c]).astype(BF16)
        give_near(net)
    ring(0, 0)
    for net in range(2):
        first_came(net, 1)
        give_far(net)
    ring(0, 1)

    for i in range(8):
        lanes = slice((i % 4) * HD, (i % 4 + 1) * HD)
        new_master[i // 4, :, lanes] = master[i // 4, :, lanes] - ortho[position[i], c]
    ring(1, 0)
    for net in range(2):
        first_came(net, 2)
    ring(0, 2)
    ring(2, 0)

    def inverse_rms():
        mean = jnp.sum(squares[...], axis=1, keepdims=True) / d_model
        squares[...] = jnp.broadcast_to(lax.rsqrt(mean + rms_epsilon), squares.shape)

    def normalise(src, offset, k):
        tile = 32 if count % 32 == 0 else 16
        first = at(X, offset, 4) * blocks

        def body(i, _):
            r = pl.ds(pl.multiple_of(i * tile, tile), tile)
            inverse = squares[r]
            for j in range(blocks):
                v = src[r, j * HD : (j + 1) * HD].astype(F32)
                v = v * inverse * gain[pl.ds(first + j, 1), :]
                normed[first + j, c, r] = v.astype(BF16)
            return 0

        lax.fori_loop(0, count // tile, body, 0)
        made = normed.at[pl.ds(first, blocks), c]
        send(made, made, pair(3 + k), partner)

    def partner_normed(offset, k):
        first = at(X, offset, 4) * blocks
        arrived(normed.at[pl.ds(first, blocks), 1 - c], pair(3 + k), partner)

    def multiply(net, offset, low=0, high=n, fresh=False):
        block = at(ring_axis[net], offset, n)
        axis = axes[net][0]
        wide = []
        for o in order[low:high]:
            across = at(axis, o, n)
            feature = block * n + across if net == 0 else across * n + block
            wide.append(normed[feature].reshape(2 * count, HD))
        rhs = weights[net, block, low:high].reshape((high - low) * HD, HD)
        product = dot(jnp.concatenate(wide, axis=1), rhs)
        total[net] = product if fresh else total[net] + product

    def tokens_one():
        arrived(came_tokens.at[0, lower], tok(2), right)
        add_squares(came_tokens.at[0], False)

    def tokens_three():
        arrived(came_tokens.at[2, upper], tok(3), left)
        add_squares(came_tokens.at[2], False)

    def tokens_two():
        arrived(came_tokens.at[1, upper], tok(4), right)
        arrived(came_tokens.at[1, lower], tok(5), left)
        add_squares(came_tokens.at[1], False)
        inverse_rms()

    def own_block():
        for k, offset in enumerate((0, -1, 1, 2)):
            partner_normed(offset, k)
        for net in range(2):
            multiply(net, 0, fresh=True)

    def distance(k):
        for net in range(2):
            for g in range(3):
                for way in range(2):
                    need(net, way, k - 1, g)
            multiply(net, k)
            multiply(net, -k)

    work = [
        (lambda: ring(1, 1), tokens_one, lambda: settle(40)),
        (lambda: ring(3, 0), tokens_three, tokens_two, lambda: settle(30)),
        (lambda: ring(1, 2), lambda: normalise(tokens, 0, 0), lambda: normalise(came_tokens.at[0], -1, 1)),
        (lambda: ring(2, 1), lambda: normalise(came_tokens.at[2], 1, 2),
         lambda: normalise(came_tokens.at[1], 2, 3), lambda: settle(24)),
        (lambda: ring(2, 2), own_block),
        (lambda: ring(3, 1), lambda: ring(3, 2)),
    ]
    for tasks in work:
        for task in tasks:
            task()
    for k in range(1, half):
        distance(k)
        if k + 1 < half:
            settle(14)

    for net in range(2):
        for g in (0, 1, 2):
            for way in range(2):
                need(net, way, half - 1, g)
        multiply(net, half)
        kv_send[net] = total[net, pl.ds(pl.multiple_of((1 - c) * count, 16), count)].astype(BF16)
        send(kv_send.at[net], kv_blocks.at[2 * c + net], pair(7 + net), partner)
    for net in range(2):
        kv_blocks[2 * c + net] = total[net, pl.ds(pl.multiple_of(c * count, 16), count)].astype(BF16)
    settle(0)
    for net in range(2):
        arrived(kv_blocks.at[2 * (1 - c) + net], pair(7 + net), partner)
    for k in range(4):
        key_values[:, k * HD : (k + 1) * HD] = kv_blocks[k]


def hand_over(*refs):
    given, taken, done = refs[:3], refs[3:6], refs[6]
    copies = [pltpu.make_async_copy(a, b, done.at[k]) for k, (a, b) in enumerate(zip(given, taken))]
    for copy in copies:
        copy.start()
    for copy in copies:
        copy.wait()


def per_device(n, d_model, master, momentum, gradient, bucket_table, tokens, norm_gain):
    height = master.shape[1]
    count, width = tokens.shape
    blocks = width // HD
    rows = PACKED // n
    half = n // 2
    hbm, anywhere, vmem = (pl.BlockSpec(memory_space=m) for m in (pltpu.HBM, pl.ANY, pltpu.VMEM))
    dma = pltpu.SemaphoreType.DMA
    scratch = [
        pltpu.SMEM(bucket_table.shape, jnp.int32),
        *[pltpu.VMEM(master.shape, F32) for _ in range(3)],
        pltpu.VMEM(tokens.shape, BF16),
        pltpu.VMEM((4 * blocks, HD), F32),
        dma((6,)),
        pltpu.VMEM((8, height, HD), F32),
        pltpu.VMEM((8, height, HD), F32),
        pltpu.VMEM((4, height, HD), F32),
        pltpu.VMEM((4, height, HD), F32),
        pltpu.VMEM((2, height, HD), F32),
        pltpu.VMEM((2, PACKED, HD), F32),
        pltpu.VMEM((2, n - 1, rows, HD), F32),
        pltpu.VMEM((2, rows, HD), F32),
        pltpu.VMEM((2, n - 1, rows, HD), F32),
        pltpu.VMEM((2, PACKED, HD), F32),
        pltpu.VMEM((8, 2, height, HD), F32),
        pltpu.VMEM((2, n, n, 2, height, HD), BF16),
        pltpu.VMEM((3, count, width), BF16),
        pltpu.VMEM((count, HD), F32),
        pltpu.VMEM((4 * blocks, 2, count, HD), BF16),
        pltpu.VMEM((2, 2 * count, HD), F32),
        pltpu.VMEM((2, count, HD), BF16),
        pltpu.VMEM((4, count, HD), BF16),
        dma((10,)),
        dma((10,)),
        dma((3, 2, 2, n - 1)),
        dma((3, 2, 2, n - 1)),
        dma((6,)),
        dma((6,)),
        dma((2, n)),
        dma((2, n)),
        dma((2, 2, half, 3)),
        dma((2, 2, half, 3)),
    ]
    outs = (
        jax.ShapeDtypeStruct(master.shape, F32),
        jax.ShapeDtypeStruct(master.shape, F32),
        jax.ShapeDtypeStruct((count, 4 * HD), BF16),
    )
    made = pl.pallas_call(
        functools.partial(kernel, n, d_model),
        out_shape=outs,
        in_specs=[hbm] * 6,
        out_specs=(vmem,) * 3,
        scratch_shapes=scratch,
        compiler_params=pltpu.CompilerParams(
            collective_id=0, has_side_effects=True, vmem_limit_bytes=48 * 1024 * 1024
        ),
    )(*(
        pltpu.with_memory_space_constraint(a, pltpu.HBM)
        for a in (bucket_table, master, momentum, gradient, tokens, norm_gain.reshape(-1, HD))
    ))
    return pl.pallas_call(
        hand_over,
        out_shape=outs,
        in_specs=[vmem] * 3,
        out_specs=(hbm,) * 3,
        scratch_shapes=[dma((3,))],
        compiler_params=pltpu.CompilerParams(vmem_limit_bytes=4 * 1024 * 1024),
    )(*made)


def solution(mesh):
    n = math.isqrt(mesh.shape["dp"] // 2)
    torus = Mesh(
        mesh.devices.reshape(n, n, 2, mesh.shape["tensor"]), ("dp_0", "dp_1", "dp_2", "tensor")
    )

    def whole(*args):
        return jax.shard_map(
            functools.partial(per_device, n, args[0].shape[1]),
            mesh=torus,
            in_specs=(
                P(None, DP, "tensor"),
                P(None, DP, "tensor"),
                P(None, DP, "tensor"),
                P("tensor", None),
                P(DP, "tensor"),
                P(),
            ),
            out_specs=(P(None, DP, "tensor"), P(None, DP, "tensor"), P(DP, "tensor")),
            check_vma=False,
        )(*args)

    return whole
```

```python
import functools
import math

import jax
import jax.numpy as jnp
from jax import lax
from jax.experimental import pallas as pl
from jax.experimental.pallas import tpu as pltpu
from jax.sharding import Mesh
from jax.sharding import PartitionSpec as P

HD = 128
NS_ITERS = 3
DP = ("dp_0", "dp_1", "dp_2")

beta_momentum = 0.95
learn_rate = 0.05
first_coeff = 3.4445
cube_coeff = -4.775
fifth_coeff = 2.0315
frob_epsilon = 1e-07
rms_epsilon = 1e-05

F32 = jnp.float32
BF16 = jnp.bfloat16
Y, Z, C, X = "dp_1", "dp_0", "dp_2", "tensor"
PACKED = 2 * HD + 64


def near_first(n):
    offsets = [0]
    for k in range(1, n // 2):
        offsets += [k, -k]
    return [*offsets, n // 2]


def split(a):
    high = a.astype(BF16)
    return high, (a - high.astype(F32)).astype(BF16)


def dot(a, b):
    return jnp.dot(a, b, preferred_element_type=F32)


def dot3(a, b):
    return dot(a[0], b[0]) + (dot(a[0], b[1]) + dot(a[1], b[0]))


def kernel(n, d_model, table_in, master_in, momentum_in, gradient_in, tokens_in, gain_in, new_master,
           new_momentum, key_values, table, master, momentum, gradient, tokens, gain, load, update,
           stacked, other_rows, heads, other_heads, packed, came1, part, came2, gram, ortho, weights,
           came_tokens, squares, normed, total, pair_send, pair_recv, gram_send,
           gram_recv, token_send, token_recv, first_send, first_recv, core_send, core_recv, ring_send,
           ring_recv):
    half = n // 2
    rows = PACKED // n
    count = tokens.shape[0]
    blocks = tokens.shape[1] // HD
    height = master.shape[1]
    z, y, c, x = (lax.axis_index(a) for a in (Z, Y, C, X))
    axes = ((Y, Z), (Z, Y))
    place = {Y: y, Z: z}
    sent, ended = [], [0]

    def at(axis, offset, size):
        here = {Y: y, Z: z, X: x}[axis]
        return lax.rem(here + (offset + size), size)

    def send(src, dst, sems, to):
        copy = pltpu.make_async_remote_copy(
            src_ref=src, dst_ref=dst, send_sem=sems[0], recv_sem=sems[1],
            device_id=to, device_id_type=pl.DeviceIdType.MESH,
        )
        copy.start()
        sent.append(copy)

    def arrived(ref, sems, to):
        pltpu.make_async_remote_copy(
            src_ref=ref, dst_ref=ref, send_sem=sems[0], recv_sem=sems[1],
            device_id=to, device_id_type=pl.DeviceIdType.MESH,
        ).wait_recv()

    def settle(mark):
        for copy in sent[ended[0] : mark]:
            copy.wait_send()
        ended[0] = max(ended[0], mark)

    partner = {C: 1 - c}

    barrier = pltpu.get_barrier_semaphore()
    greeted = [partner, {X: at(X, 1, 4)}, {X: at(X, -1, 4)}]
    for axis in (Y, Z):
        greeted += [{axis: at(axis, d, n)} for d in range(1, n)]
    for device in greeted:
        pl.semaphore_signal(barrier, inc=1, device_id=device, device_id_type=pl.DeviceIdType.MESH)

    loads = [
        pltpu.make_async_copy(src, dst, load.at[k])
        for k, (src, dst) in enumerate((
            (table_in, table), (gradient_in, gradient), (momentum_in, momentum),
            (master_in, master), (tokens_in, tokens), (gain_in, gain),
        ))
    ]
    for copy in loads:
        copy.start()
    loads[0].wait()

    bucket = [table[0, i] for i in range(8)]
    position = []
    for i in range(8):
        earlier = jnp.int32(0)
        for j in range(i):
            earlier += jnp.where(bucket[j] == bucket[i], 1, 0)
        position.append(2 * bucket[i] + earlier)
    held = []
    for s in range(8):
        which = jnp.int32(0)
        for i in range(8):
            which += jnp.where(position[i] == s, i, 0)
        held.append(which)

    for copy in loads[1:4]:
        copy.wait()
    for layer in range(2):
        for slot in range(4):
            lanes = slice(slot * HD, (slot + 1) * HD)
            g = gradient[layer, :, lanes]
            m = beta_momentum * momentum[layer, :, lanes] + g
            new_momentum[layer, :, lanes] = m
            update[layer * 4 + slot] = g + beta_momentum * m
            if layer == 0:
                heads[slot] = master[0, :, lanes]
    for s in range(8):
        stacked[s] = update[held[s]]

    pl.semaphore_wait(barrier, len(greeted))

    def pair(k):
        return pair_send.at[k], pair_recv.at[k]

    send(stacked.at[pl.ds(4 * (1 - c), 4)], other_rows, pair(0), partner)
    send(heads.at[pl.ds(2 * (1 - c), 2)], other_heads, pair(1), partner)

    right, left = {X: at(X, 1, 4)}, {X: at(X, -1, 4)}
    upper, lower = pl.ds(0, count // 2), pl.ds(count // 2, count // 2)

    for copy in loads[4:]:
        copy.wait()

    def tok(k):
        return token_send.at[k], token_recv.at[k]

    send(tokens.at[upper], came_tokens.at[0, upper], tok(0), right)
    send(tokens.at[lower], came_tokens.at[2, lower], tok(1), left)
    send(tokens.at[lower], came_tokens.at[0, lower], tok(2), right)
    send(tokens.at[upper], came_tokens.at[2, upper], tok(3), left)

    arrived(other_rows, pair(0), partner)

    def chip_rows(b):
        own = jnp.concatenate([stacked[4 * c + 2 * b], stacked[4 * c + 2 * b + 1]], axis=1)
        other = jnp.concatenate([other_rows[2 * b], other_rows[2 * b + 1]], axis=1)
        return jnp.concatenate([own, other], axis=0)

    parts = ((0, 16), (16, rows))

    def lines(ref, net, chunk, p):
        low, high = parts[p]
        return ref.at[net, pl.ds(pl.multiple_of(chunk * rows + low, 8), high - low)]

    def some(ref, net, d, p):
        low, high = parts[p]
        return ref.at[net, d - 1, pl.ds(low, high - low)]

    far_first = [o % n for o in reversed(near_first(n)[1:])]

    def gsem(stage, net, p, d):
        return gram_send.at[stage, net, p, d - 1], gram_recv.at[stage, net, p, d - 1]

    r_id = lax.broadcasted_iota(jnp.int32, (HD, HD), 0)
    c_id = lax.broadcasted_iota(jnp.int32, (HD, HD), 1)
    for net in range(2):
        s = chip_rows(net)
        g = dot3(split(s.T), split(s))
        second = g[HD:, HD:]
        packed[net, 0:HD] = jnp.where(r_id <= c_id, g[:HD, :HD], second)
        packed[net, HD : 2 * HD] = g[:HD, HD:]
        diagonal = jnp.sum(jnp.where(r_id == c_id, second, 0.0), axis=0, keepdims=True)
        packed[net, 2 * HD :] = jnp.broadcast_to(diagonal, (PACKED - 2 * HD, HD))
    for p in range(2):
        for net in range(2):
            axis = axes[net][0]
            for d in far_first:
                to = at(axis, d, n)
                send(lines(packed, net, to, p), some(came1, net, d, p), gsem(0, net, p, d), {axis: to})

    def add_squares(src, fresh):
        tile = 32 if count % 32 == 0 else 16

        def body(i, _):
            r = pl.ds(pl.multiple_of(i * tile, tile), tile)
            t = jnp.zeros((tile, HD), F32) if fresh else squares[r]
            for j in range(blocks):
                v = src[r, j * HD : (j + 1) * HD].astype(F32)
                t = t + v * v
            squares[r] = t
            return 0

        lax.fori_loop(0, count // tile, body, 0)

    add_squares(tokens, True)

    for p, (low, high) in enumerate(parts):
        for net in range(2):
            axis, other = axes[net]
            for d in range(1, n):
                arrived(some(came1, net, d, p), gsem(0, net, p, d), {axis: at(axis, d, n)})
            t = lines(packed, net, place[axis], p)[...]
            for d in range(1, n):
                t = t + came1[net, d - 1, low:high]
            part[net, low:high] = t
            for d in far_first:
                send(part.at[net, pl.ds(low, high - low)], some(came2, net, d, p), gsem(1, net, p, d),
                     {other: at(other, d, n)})
    for p, (low, high) in enumerate(parts):
        for net in range(2):
            axis, other = axes[net]
            for d in range(1, n):
                arrived(some(came2, net, d, p), gsem(1, net, p, d), {other: at(other, d, n)})
            t = part[net, low:high]
            for d in range(1, n):
                t = t + came2[net, d - 1, low:high]
            own = lines(gram, net, place[axis], p)
            own[...] = t
            for d in far_first:
                send(own, own, gsem(2, net, p, d), {axis: at(axis, d, n)})

    arrived(came_tokens.at[0, upper], tok(0), right)
    send(came_tokens.at[0, upper], came_tokens.at[1, upper], tok(4), right)
    arrived(came_tokens.at[2, lower], tok(1), left)
    send(came_tokens.at[2, lower], came_tokens.at[1, lower], tok(5), left)

    for net in range(2):
        axis = axes[net][0]
        for p in range(2):
            for d in range(1, n):
                arrived(lines(gram, net, at(axis, -d, n), p), gsem(2, net, p, d), {axis: at(axis, d, n)})

    eye = jnp.where(
        lax.broadcasted_iota(jnp.int32, (2 * HD, 2 * HD), 0)
        == lax.broadcasted_iota(jnp.int32, (2 * HD, 2 * HD), 1), 1.0, 0.0
    ).astype(F32)
    step = learn_rate * math.sqrt(max(1.0, d_model / (2.0 * HD)))
    grams, ortho_rows = [], []
    for net in range(2):
        both, corner = gram[net, 0:HD], gram[net, HD : 2 * HD]
        turned = both.T
        one = jnp.where(r_id <= c_id, both, turned)
        two = jnp.where(r_id > c_id, both, jnp.where(r_id < c_id, turned, gram[net, 2 * HD : 2 * HD + 1]))
        top = jnp.concatenate([one, corner], axis=1)
        bottom = jnp.concatenate([corner.T, two], axis=1)
        g = jnp.concatenate([top, bottom], axis=0)
        trace = jnp.sum(jnp.sum(g * eye, axis=1, keepdims=True), axis=0, keepdims=True)
        scale = 1.0 / (jnp.sqrt(trace) + frob_epsilon)
        grams.append(g * (scale * scale))
        ortho_rows.append(chip_rows(net) * scale)
    for iteration in range(NS_ITERS):
        gs = [split(g) for g in grams]
        squared = [dot3(g, g) for g in gs]
        factor = [
            first_coeff * eye + (cube_coeff * g + fifth_coeff * q) for g, q in zip(grams, squared)
        ]
        fs = [split(f) for f in factor]
        if iteration + 1 < NS_ITERS:
            half_way = [dot3(f, g) for f, g in zip(fs, gs)]
            grams = [dot3(split(h), f) for h, f in zip(half_way, fs)]
            ortho_rows = [dot3(split(o), f) for o, f in zip(ortho_rows, fs)]

    for net in range(2):
        moved = dot3(split(ortho_rows[net]), fs[net]) * step
        for h in range(2):
            lanes = slice(h * HD, (h + 1) * HD)
            ortho[4 * c + 2 * net + h, c] = moved[:height, lanes]
            ortho[4 * c + 2 * net + h, 1 - c] = moved[height:, lanes]
        mine = ortho.at[pl.ds(4 * c + 2 * net, 2)]
        send(mine, mine, pair(2 + net), partner)
    arrived(other_heads, pair(1), partner)
    for net in range(2):
        arrived(ortho.at[pl.ds(4 * (1 - c) + 2 * net, 2)], pair(2 + net), partner)

    order = near_first(n)
    slot_of = {o % n: k for k, o in enumerate(order)}
    ring_axis = (Z, Y)

    near = n // 4
    groups = ((0, 1), (1, 2 * near + 1), (2 * near + 1, n))

    def rsem(net, way, s, g):
        return ring_send.at[net, way, s, g], ring_recv.at[net, way, s, g]

    def fsem(net, k):
        return first_send.at[net, k], first_recv.at[net, k]

    def sub(net, offset, g, core=c):
        low, high = groups[g]
        return weights.at[core, net, at(ring_axis[net], offset, n), pl.ds(low, high - low)]

    def piece(net, k):
        return weights.at[c, net, place[ring_axis[net]], k]

    def give(net, target, source, to):
        k = slot_of[target % n]
        send(piece(net, source), piece(net, k), fsem(net, k), {axes[net][0]: at(axes[net][0], to, n)})

    def give_near(net):
        for t in range(1, near + 1):
            give(net, t, 0, -t)
            give(net, -t, 0, t)

    def give_far(net):
        ahead, behind = slot_of[near % n], slot_of[-near % n]
        for t in range(near + 1, half):
            give(net, t, ahead, near - t)
            give(net, -t, behind, t - near)
        give(net, half, jnp.where(c == 0, ahead, behind), (2 * c - 1) * (half - near))

    def first_came(net, g):
        if groups[g][0] < groups[g][1]:
            fresh.append((net, 0, g))
        for k in range(*groups[g]):
            arrived(piece(net, k), fsem(net, k), {axes[net][0]: at(axes[net][0], 1, n)})

    def csem(net, offset, g):
        return core_send.at[net, offset % n, g], core_recv.at[net, offset % n, g]

    fresh = []

    def share():
        while fresh:
            net, offset, g = fresh.pop(0)
            moving = sub(net, offset, g)
            send(moving, moving, csem(net, offset, g), partner)

    def shared(net, offset):
        for g, (low, high) in enumerate(groups):
            if low < high:
                arrived(sub(net, offset, g, 1 - c), csem(net, offset, g), partner)

    def goes(way, s, g):
        low, high = groups[g]
        return low < high and (s + 1 < half or way == g % 2)

    seen = set()

    def need(net, way, s, g):
        if (net, way, s, g) in seen or not goes(way, s, g):
            return
        seen.add((net, way, s, g))
        sign = 1 if way == 0 else -1
        arrived(sub(net, -sign * (s + 1), g), rsem(net, way, s, g),
                {ring_axis[net]: at(ring_axis[net], sign, n)})
        fresh.append((net, -sign * (s + 1), g))

    def ring(s, g):
        if s >= half:
            return
        for net in range(2):
            for way, sign in enumerate((1, -1)):
                if goes(way, s, g):
                    if s > 0:
                        need(net, way, s - 1, g)
                    moving = sub(net, -sign * s, g)
                    send(moving, moving, rsem(net, way, s, g),
                         {ring_axis[net]: at(ring_axis[net], sign, n)})
        share()

    marks = [len(sent)]
    for net in range(2):
        where = jnp.where(c == 0, position[net], position[2 + net])
        block = place[ring_axis[net]]
        weights[c, net, block, 0, c] = (heads[2 * c + net] - ortho[where, c]).astype(BF16)
        weights[c, net, block, 0, 1 - c] = (other_heads[net] - ortho[where, 1 - c]).astype(BF16)
        give_near(net)
        fresh.append((net, 0, 0))
    ring(0, 0)
    for net in range(2):
        first_came(net, 1)
        give_far(net)
    ring(0, 1)
    marks.append(len(sent))

    for i in range(8):
        lanes = slice((i % 4) * HD, (i % 4 + 1) * HD)
        new_master[i // 4, :, lanes] = master[i // 4, :, lanes] - ortho[position[i], c]
    ring(1, 0)
    for net in range(2):
        first_came(net, 2)
    ring(0, 2)
    ring(2, 0)

    def inverse_rms():
        mean = jnp.sum(squares[...], axis=1, keepdims=True) / d_model
        squares[...] = jnp.broadcast_to(lax.rsqrt(mean + rms_epsilon), squares.shape)

    def normalise(src, offset):
        tile = 32 if count % 32 == 0 else 16
        first = at(X, offset, 4) * blocks

        def body(i, _):
            r = pl.ds(pl.multiple_of(i * tile, tile), tile)
            inverse = squares[r]
            for j in range(blocks):
                v = src[r, j * HD : (j + 1) * HD].astype(F32)
                v = v * inverse * gain[pl.ds(first + j, 1), :]
                normed[first + j, r] = v.astype(BF16)
            return 0

        lax.fori_loop(0, count // tile, body, 0)
    def multiply(net, offset, first=False):
        shared(net, offset)
        block = at(ring_axis[net], offset, n)
        axis = axes[net][0]
        wide = []
        for o in order:
            across = at(axis, o, n)
            wide.append(normed[block * n + across if net == 0 else across * n + block])
        tall = [weights[core, net, block].reshape(n * HD, HD) for core in range(2)]
        product = dot(jnp.concatenate(wide, axis=1), jnp.concatenate(tall, axis=1))
        total[net] = product if first else total[net] + product

    def tokens_one():
        arrived(came_tokens.at[0, lower], tok(2), right)
        add_squares(came_tokens.at[0], False)

    def tokens_three():
        arrived(came_tokens.at[2, upper], tok(3), left)
        add_squares(came_tokens.at[2], False)

    def tokens_two():
        arrived(came_tokens.at[1, upper], tok(4), right)
        arrived(came_tokens.at[1, lower], tok(5), left)
        add_squares(came_tokens.at[1], False)
        inverse_rms()

    def own_block():
        for net in range(2):
            multiply(net, 0, True)

    def distance(k):
        for net in range(2):
            for g in range(3):
                for way in range(2):
                    need(net, way, k - 1, g)
        share()
        for net in range(2):
            multiply(net, k)
            if k < half:
                multiply(net, -k)

    work = (
        (lambda: ring(1, 1), tokens_one, lambda: settle(marks[0]), lambda: marks.append(len(sent))),
        (lambda: ring(3, 0), tokens_three),
        (lambda: ring(1, 2), tokens_two, lambda: normalise(tokens, 0), lambda: settle(marks[1])),
        (lambda: ring(2, 1), lambda: marks.append(len(sent)), lambda: normalise(came_tokens.at[0], -1),
         lambda: normalise(came_tokens.at[2], 1), lambda: normalise(came_tokens.at[1], 2)),
        (lambda: ring(2, 2), own_block, functools.partial(distance, 1) if half > 1 else share),
        (lambda: ring(3, 1), lambda: settle(marks[2]), lambda: ring(3, 2)),
    )
    for tasks in work:
        for task in tasks:
            task()
    for k in range(2, half):
        distance(k)
    settle(marks[3])
    distance(half)
    for net in range(2):
        for core in range(2):
            columns = slice((2 * core + net) * HD, (2 * core + net + 1) * HD)
            key_values[:, columns] = total[net, :, core * HD : (core + 1) * HD].astype(BF16)
    settle(len(sent))


def hand_over(*refs):
    given, taken, done = refs[:3], refs[3:6], refs[6]
    copies = [pltpu.make_async_copy(a, b, done.at[k]) for k, (a, b) in enumerate(zip(given, taken))]
    for copy in copies:
        copy.start()
    for copy in copies:
        copy.wait()


def per_device(n, d_model, master, momentum, gradient, bucket_table, tokens, norm_gain):
    height = master.shape[1]
    count, width = tokens.shape
    blocks = width // HD
    rows = PACKED // n
    half = n // 2
    hbm, anywhere, vmem = (pl.BlockSpec(memory_space=m) for m in (pltpu.HBM, pl.ANY, pltpu.VMEM))
    dma = pltpu.SemaphoreType.DMA
    scratch = [
        pltpu.SMEM(bucket_table.shape, jnp.int32),
        *[pltpu.VMEM(master.shape, F32) for _ in range(3)],
        pltpu.VMEM(tokens.shape, BF16),
        pltpu.VMEM((4 * blocks, HD), F32),
        dma((6,)),
        pltpu.VMEM((8, height, HD), F32),
        pltpu.VMEM((8, height, HD), F32),
        pltpu.VMEM((4, height, HD), F32),
        pltpu.VMEM((4, height, HD), F32),
        pltpu.VMEM((2, height, HD), F32),
        pltpu.VMEM((2, PACKED, HD), F32),
        pltpu.VMEM((2, n - 1, rows, HD), F32),
        pltpu.VMEM((2, rows, HD), F32),
        pltpu.VMEM((2, n - 1, rows, HD), F32),
        pltpu.VMEM((2, PACKED, HD), F32),
        pltpu.VMEM((8, 2, height, HD), F32),
        pltpu.VMEM((2, 2, n, n, 2, height, HD), BF16),
        pltpu.VMEM((3, count, width), BF16),
        pltpu.VMEM((count, HD), F32),
        pltpu.VMEM((4 * blocks, count, HD), BF16),
        pltpu.VMEM((2, count, 2 * HD), F32),
        dma((4,)),
        dma((4,)),
        dma((3, 2, 2, n - 1)),
        dma((3, 2, 2, n - 1)),
        dma((6,)),
        dma((6,)),
        dma((2, n)),
        dma((2, n)),
        dma((2, n, 3)),
        dma((2, n, 3)),
        dma((2, 2, half, 3)),
        dma((2, 2, half, 3)),
    ]
    outs = (
        jax.ShapeDtypeStruct(master.shape, F32),
        jax.ShapeDtypeStruct(master.shape, F32),
        jax.ShapeDtypeStruct((count, 4 * HD), BF16),
    )
    made = pl.pallas_call(
        functools.partial(kernel, n, d_model),
        out_shape=outs,
        in_specs=[hbm] * 6,
        out_specs=(vmem,) * 3,
        scratch_shapes=scratch,
        compiler_params=pltpu.CompilerParams(
            collective_id=0, has_side_effects=True, vmem_limit_bytes=48 * 1024 * 1024
        ),
    )(*(
        pltpu.with_memory_space_constraint(a, pltpu.HBM)
        for a in (bucket_table, master, momentum, gradient, tokens, norm_gain.reshape(-1, HD))
    ))
    return pl.pallas_call(
        hand_over,
        out_shape=outs,
        in_specs=[vmem] * 3,
        out_specs=(hbm,) * 3,
        scratch_shapes=[dma((3,))],
        compiler_params=pltpu.CompilerParams(vmem_limit_bytes=4 * 1024 * 1024),
    )(*made)


def solution(mesh):
    n = math.isqrt(mesh.shape["dp"] // 2)
    torus = Mesh(
        mesh.devices.reshape(n, n, 2, mesh.shape["tensor"]), ("dp_0", "dp_1", "dp_2", "tensor")
    )

    def whole(*args):
        return jax.shard_map(
            functools.partial(per_device, n, args[0].shape[1]),
            mesh=torus,
            in_specs=(
                P(None, DP, "tensor"),
                P(None, DP, "tensor"),
                P(None, DP, "tensor"),
                P("tensor", None),
                P(DP, "tensor"),
                P(),
            ),
            out_specs=(P(None, DP, "tensor"), P(None, DP, "tensor"), P(DP, "tensor")),
            check_vma=False,
        )(*args)

    return whole
```

```python
import functools
import math

import jax
import jax.numpy as jnp
from jax import lax
from jax.experimental import pallas as pl
from jax.experimental.pallas import tpu as pltpu
from jax.sharding import Mesh
from jax.sharding import PartitionSpec as P

HD = 128
NS_ITERS = 3
DP = ("dp_0", "dp_1", "dp_2")

beta_momentum = 0.95
learn_rate = 0.05
first_coeff = 3.4445
cube_coeff = -4.775
fifth_coeff = 2.0315
frob_epsilon = 1e-07
rms_epsilon = 1e-05

F32 = jnp.float32
BF16 = jnp.bfloat16
Y, Z, C, X = "dp_1", "dp_0", "dp_2", "tensor"
PACKED = 2 * HD + 64


def near_first(n):
    offsets = [0]
    for k in range(1, n // 2):
        offsets += [k, -k]
    return [*offsets, n // 2]


def split(a):
    high = a.astype(BF16)
    return high, (a - high.astype(F32)).astype(BF16)


def dot(a, b):
    return jnp.dot(a, b, preferred_element_type=F32)


def dot3(a, b):
    return dot(a[0], b[0]) + (dot(a[0], b[1]) + dot(a[1], b[0]))


def kernel(n, d_model, table_in, master_in, momentum_in, gradient_in, tokens_in, gain_in, new_master,
           new_momentum, key_values, table, master, momentum, gradient, tokens, gain, load, update,
           stacked, other_rows, heads, other_heads, packed, came1, part, came2, gram, ortho, weights,
           came_tokens, squares, normed, total, pair_send, pair_recv, gram_send,
           gram_recv, token_send, token_recv, first_send, first_recv, core_send, core_recv, ring_send,
           ring_recv):
    half = n // 2
    rows = PACKED // n
    count = tokens.shape[0]
    blocks = tokens.shape[1] // HD
    height = master.shape[1]
    z, y, c, x = (lax.axis_index(a) for a in (Z, Y, C, X))
    axes = ((Y, Z), (Z, Y))
    place = {Y: y, Z: z}
    sent, ended = [], [0]

    def at(axis, offset, size):
        here = {Y: y, Z: z, X: x}[axis]
        return lax.rem(here + (offset + size), size)

    def send(src, dst, sems, to):
        copy = pltpu.make_async_remote_copy(
            src_ref=src, dst_ref=dst, send_sem=sems[0], recv_sem=sems[1],
            device_id=to, device_id_type=pl.DeviceIdType.MESH,
        )
        copy.start()
        sent.append(copy)

    def arrived(ref, sems, to):
        pltpu.make_async_remote_copy(
            src_ref=ref, dst_ref=ref, send_sem=sems[0], recv_sem=sems[1],
            device_id=to, device_id_type=pl.DeviceIdType.MESH,
        ).wait_recv()

    def settle(mark):
        for copy in sent[ended[0] : mark]:
            copy.wait_send()
        ended[0] = max(ended[0], mark)

    partner = {C: 1 - c}

    barrier = pltpu.get_barrier_semaphore()
    greeted = [partner, {X: at(X, 1, 4)}, {X: at(X, -1, 4)}]
    for axis in (Y, Z):
        greeted += [{axis: at(axis, d, n)} for d in range(1, n)]
    for device in greeted:
        pl.semaphore_signal(barrier, inc=1, device_id=device, device_id_type=pl.DeviceIdType.MESH)

    loads = [
        pltpu.make_async_copy(src, dst, load.at[k])
        for k, (src, dst) in enumerate((
            (table_in, table), (gradient_in, gradient), (momentum_in, momentum),
            (master_in, master), (tokens_in, tokens), (gain_in, gain),
        ))
    ]
    for copy in loads:
        copy.start()
    loads[0].wait()

    bucket = [table[0, i] for i in range(8)]
    position = []
    for i in range(8):
        earlier = jnp.int32(0)
        for j in range(i):
            earlier += jnp.where(bucket[j] == bucket[i], 1, 0)
        position.append(2 * bucket[i] + earlier)
    held = []
    for s in range(8):
        which = jnp.int32(0)
        for i in range(8):
            which += jnp.where(position[i] == s, i, 0)
        held.append(which)

    for copy in loads[1:4]:
        copy.wait()
    for layer in range(2):
        for slot in range(4):
            lanes = slice(slot * HD, (slot + 1) * HD)
            g = gradient[layer, :, lanes]
            m = beta_momentum * momentum[layer, :, lanes] + g
            new_momentum[layer, :, lanes] = m
            update[layer * 4 + slot] = g + beta_momentum * m
            if layer == 0:
                heads[slot] = master[0, :, lanes]
    for s in range(8):
        stacked[s] = update[held[s]]

    pl.semaphore_wait(barrier, len(greeted))

    def pair(k):
        return pair_send.at[k], pair_recv.at[k]

    send(stacked.at[pl.ds(4 * (1 - c), 4)], other_rows, pair(0), partner)
    send(heads.at[pl.ds(2 * (1 - c), 2)], other_heads, pair(1), partner)

    right, left = {X: at(X, 1, 4)}, {X: at(X, -1, 4)}
    upper, lower = pl.ds(0, count // 2), pl.ds(count // 2, count // 2)

    for copy in loads[4:]:
        copy.wait()

    def tok(k):
        return token_send.at[k], token_recv.at[k]

    send(tokens.at[upper], came_tokens.at[0, upper], tok(0), right)
    send(tokens.at[lower], came_tokens.at[2, lower], tok(1), left)
    send(tokens.at[lower], came_tokens.at[0, lower], tok(2), right)
    send(tokens.at[upper], came_tokens.at[2, upper], tok(3), left)

    arrived(other_rows, pair(0), partner)

    def chip_rows(b):
        own = jnp.concatenate([stacked[4 * c + 2 * b], stacked[4 * c + 2 * b + 1]], axis=1)
        other = jnp.concatenate([other_rows[2 * b], other_rows[2 * b + 1]], axis=1)
        return jnp.concatenate([own, other], axis=0)

    parts = ((0, 16), (16, rows))

    def lines(ref, net, chunk, p):
        low, high = parts[p]
        return ref.at[net, pl.ds(pl.multiple_of(chunk * rows + low, 8), high - low)]

    def some(ref, net, d, p):
        low, high = parts[p]
        return ref.at[net, d - 1, pl.ds(low, high - low)]

    far_first = [o % n for o in reversed(near_first(n)[1:])]

    def gsem(stage, net, p, d):
        return gram_send.at[stage, net, p, d - 1], gram_recv.at[stage, net, p, d - 1]

    r_id = lax.broadcasted_iota(jnp.int32, (HD, HD), 0)
    c_id = lax.broadcasted_iota(jnp.int32, (HD, HD), 1)
    for net in range(2):
        s = chip_rows(net)
        g = dot3(split(s.T), split(s))
        second = g[HD:, HD:]
        packed[net, 0:HD] = jnp.where(r_id <= c_id, g[:HD, :HD], second)
        packed[net, HD : 2 * HD] = g[:HD, HD:]
        diagonal = jnp.sum(jnp.where(r_id == c_id, second, 0.0), axis=0, keepdims=True)
        packed[net, 2 * HD :] = jnp.broadcast_to(diagonal, (PACKED - 2 * HD, HD))
    for p in range(2):
        for net in range(2):
            axis = axes[net][0]
            for d in far_first:
                to = at(axis, d, n)
                send(lines(packed, net, to, p), some(came1, net, d, p), gsem(0, net, p, d), {axis: to})

    def add_squares(src, fresh):
        tile = 32 if count % 32 == 0 else 16

        def body(i, _):
            r = pl.ds(pl.multiple_of(i * tile, tile), tile)
            t = jnp.zeros((tile, HD), F32) if fresh else squares[r]
            for j in range(blocks):
                v = src[r, j * HD : (j + 1) * HD].astype(F32)
                t = t + v * v
            squares[r] = t
            return 0

        lax.fori_loop(0, count // tile, body, 0)

    add_squares(tokens, True)

    for p, (low, high) in enumerate(parts):
        for net in range(2):
            axis, other = axes[net]
            for d in range(1, n):
                arrived(some(came1, net, d, p), gsem(0, net, p, d), {axis: at(axis, d, n)})
            t = lines(packed, net, place[axis], p)[...]
            for d in range(1, n):
                t = t + came1[net, d - 1, low:high]
            part[net, low:high] = t
            for d in far_first:
                send(part.at[net, pl.ds(low, high - low)], some(came2, net, d, p), gsem(1, net, p, d),
                     {other: at(other, d, n)})
    for p, (low, high) in enumerate(parts):
        for net in range(2):
            axis, other = axes[net]
            for d in range(1, n):
                arrived(some(came2, net, d, p), gsem(1, net, p, d), {other: at(other, d, n)})
            t = part[net, low:high]
            for d in range(1, n):
                t = t + came2[net, d - 1, low:high]
            own = lines(gram, net, place[axis], p)
            own[...] = t
            for d in far_first:
                send(own, own, gsem(2, net, p, d), {axis: at(axis, d, n)})

    arrived(came_tokens.at[0, upper], tok(0), right)
    send(came_tokens.at[0, upper], came_tokens.at[1, upper], tok(4), right)
    arrived(came_tokens.at[2, lower], tok(1), left)
    send(came_tokens.at[2, lower], came_tokens.at[1, lower], tok(5), left)

    for net in range(2):
        axis = axes[net][0]
        for p in range(2):
            for d in range(1, n):
                arrived(lines(gram, net, at(axis, -d, n), p), gsem(2, net, p, d), {axis: at(axis, d, n)})

    eye = jnp.where(
        lax.broadcasted_iota(jnp.int32, (2 * HD, 2 * HD), 0)
        == lax.broadcasted_iota(jnp.int32, (2 * HD, 2 * HD), 1), 1.0, 0.0
    ).astype(F32)
    step = learn_rate * math.sqrt(max(1.0, d_model / (2.0 * HD)))
    grams, ortho_rows = [], []
    for net in range(2):
        both, corner = gram[net, 0:HD], gram[net, HD : 2 * HD]
        turned = both.T
        one = jnp.where(r_id <= c_id, both, turned)
        two = jnp.where(r_id > c_id, both, jnp.where(r_id < c_id, turned, gram[net, 2 * HD : 2 * HD + 1]))
        top = jnp.concatenate([one, corner], axis=1)
        bottom = jnp.concatenate([corner.T, two], axis=1)
        g = jnp.concatenate([top, bottom], axis=0)
        trace = jnp.sum(jnp.sum(g * eye, axis=1, keepdims=True), axis=0, keepdims=True)
        scale = 1.0 / (jnp.sqrt(trace) + frob_epsilon)
        grams.append(g * (scale * scale))
        ortho_rows.append(chip_rows(net) * scale)
    for iteration in range(NS_ITERS):
        gs = [split(g) for g in grams]
        squared = [dot3(g, g) for g in gs]
        factor = [
            first_coeff * eye + (cube_coeff * g + fifth_coeff * q) for g, q in zip(grams, squared)
        ]
        fs = [split(f) for f in factor]
        if iteration + 1 < NS_ITERS:
            half_way = [dot3(f, g) for f, g in zip(fs, gs)]
            grams = [dot3(split(h), f) for h, f in zip(half_way, fs)]
            ortho_rows = [dot3(split(o), f) for o, f in zip(ortho_rows, fs)]

    for net in range(2):
        moved = dot3(split(ortho_rows[net]), fs[net]) * step
        for h in range(2):
            lanes = slice(h * HD, (h + 1) * HD)
            ortho[4 * c + 2 * net + h, c] = moved[:height, lanes]
            ortho[4 * c + 2 * net + h, 1 - c] = moved[height:, lanes]
        mine = ortho.at[pl.ds(4 * c + 2 * net, 2)]
        send(mine, mine, pair(2 + net), partner)
    arrived(other_heads, pair(1), partner)
    for net in range(2):
        arrived(ortho.at[pl.ds(4 * (1 - c) + 2 * net, 2)], pair(2 + net), partner)

    order = near_first(n)
    slot_of = {o % n: k for k, o in enumerate(order)}
    ring_axis = (Z, Y)

    near = n // 4
    groups = ((0, 1), (1, 2 * near + 1), (2 * near + 1, n))

    def rsem(net, way, s, g):
        return ring_send.at[net, way, s, g], ring_recv.at[net, way, s, g]

    def fsem(net, k):
        return first_send.at[net, k], first_recv.at[net, k]

    def sub(net, offset, g, core=c):
        low, high = groups[g]
        return weights.at[core, net, at(ring_axis[net], offset, n), pl.ds(low, high - low)]

    def piece(net, k):
        return weights.at[c, net, place[ring_axis[net]], k]

    def give(net, target, source, to):
        k = slot_of[target % n]
        send(piece(net, source), piece(net, k), fsem(net, k), {axes[net][0]: at(axes[net][0], to, n)})

    def give_near(net):
        for t in range(1, near + 1):
            give(net, t, 0, -t)
            give(net, -t, 0, t)

    def give_far(net):
        ahead, behind = slot_of[near % n], slot_of[-near % n]
        for t in range(near + 1, half):
            give(net, t, ahead, near - t)
            give(net, -t, behind, t - near)
        give(net, half, jnp.where(c == 0, ahead, behind), (2 * c - 1) * (half - near))

    def first_came(net, g):
        if groups[g][0] < groups[g][1]:
            fresh.append((net, 0, g))
        for k in range(*groups[g]):
            arrived(piece(net, k), fsem(net, k), {axes[net][0]: at(axes[net][0], 1, n)})

    def csem(net, offset, g):
        return core_send.at[net, offset % n, g], core_recv.at[net, offset % n, g]

    fresh = []

    def share():
        while fresh:
            net, offset, g = fresh.pop(0)
            moving = sub(net, offset, g)
            send(moving, moving, csem(net, offset, g), partner)

    def shared(net, offset):
        for g, (low, high) in enumerate(groups):
            if low < high:
                arrived(sub(net, offset, g, 1 - c), csem(net, offset, g), partner)

    def goes(way, s, g):
        low, high = groups[g]
        return low < high and (s + 1 < half or (way == 0) == (g == 2))

    seen = set()

    def need(net, way, s, g):
        if (net, way, s, g) in seen or not goes(way, s, g):
            return
        seen.add((net, way, s, g))
        sign = 1 if way == 0 else -1
        arrived(sub(net, -sign * (s + 1), g), rsem(net, way, s, g),
                {ring_axis[net]: at(ring_axis[net], sign, n)})
        fresh.append((net, -sign * (s + 1), g))

    def skip_one():
        for net in range(2):
            for way, sign in enumerate((1, -1)):
                if half > 2:
                    own = sub(net, 0, 0)
                    send(own, own, rsem(net, way, 1, 0),
                         {ring_axis[net]: at(ring_axis[net], 2 * sign, n)})

    def ring(s, g):
        if s >= half:
            return
        for net in range(2):
            for way, sign in enumerate((1, -1)):
                if goes(way, s, g):
                    if s > 0:
                        need(net, way, s - 1, g)
                    if half > 2 and (s, g) == (1, 0):
                        continue
                    moving = sub(net, -sign * s, g)
                    send(moving, moving, rsem(net, way, s, g),
                         {ring_axis[net]: at(ring_axis[net], sign, n)})
        share()

    marks = [len(sent)]
    for net in range(2):
        where = jnp.where(c == 0, position[net], position[2 + net])
        block = place[ring_axis[net]]
        weights[c, net, block, 0, c] = (heads[2 * c + net] - ortho[where, c]).astype(BF16)
        weights[c, net, block, 0, 1 - c] = (other_heads[net] - ortho[where, 1 - c]).astype(BF16)
        give_near(net)
        fresh.append((net, 0, 0))
    ring(0, 0)
    skip_one()
    for net in range(2):
        first_came(net, 1)
        give_far(net)
    ring(0, 1)
    marks.append(len(sent))

    for i in range(8):
        lanes = slice((i % 4) * HD, (i % 4 + 1) * HD)
        new_master[i // 4, :, lanes] = master[i // 4, :, lanes] - ortho[position[i], c]
    ring(1, 0)
    for net in range(2):
        first_came(net, 2)
    ring(0, 2)
    ring(2, 0)

    def inverse_rms():
        mean = jnp.sum(squares[...], axis=1, keepdims=True) / d_model
        squares[...] = jnp.broadcast_to(lax.rsqrt(mean + rms_epsilon), squares.shape)

    def normalise(src, offset):
        tile = 32 if count % 32 == 0 else 16
        first = at(X, offset, 4) * blocks

        def body(i, _):
            r = pl.ds(pl.multiple_of(i * tile, tile), tile)
            inverse = squares[r]
            for j in range(blocks):
                v = src[r, j * HD : (j + 1) * HD].astype(F32)
                v = v * inverse * gain[pl.ds(first + j, 1), :]
                normed[first + j, r] = v.astype(BF16)
            return 0

        lax.fori_loop(0, count // tile, body, 0)
    def multiply(net, offset, first=False):
        shared(net, offset)
        block = at(ring_axis[net], offset, n)
        axis = axes[net][0]
        wide = []
        for o in order:
            across = at(axis, o, n)
            wide.append(normed[block * n + across if net == 0 else across * n + block])
        tall = [weights[core, net, block].reshape(n * HD, HD) for core in range(2)]
        product = dot(jnp.concatenate(wide, axis=1), jnp.concatenate(tall, axis=1))
        total[net] = product if first else total[net] + product

    def tokens_one():
        arrived(came_tokens.at[0, lower], tok(2), right)
        add_squares(came_tokens.at[0], False)

    def tokens_three():
        arrived(came_tokens.at[2, upper], tok(3), left)
        add_squares(came_tokens.at[2], False)

    def tokens_two():
        arrived(came_tokens.at[1, upper], tok(4), right)
        arrived(came_tokens.at[1, lower], tok(5), left)
        add_squares(came_tokens.at[1], False)
        inverse_rms()

    def own_block():
        for net in range(2):
            multiply(net, 0, True)

    def distance(k):
        for net in range(2):
            for g in range(3):
                for way in range(2):
                    need(net, way, k - 1, g)
        share()
        if k == half:
            settle(len(sent))
        for net in range(2):
            multiply(net, k)
            if k < half:
                multiply(net, -k)

    work = (
        (lambda: ring(1, 1), tokens_one, lambda: settle(marks[0]), lambda: marks.append(len(sent))),
        (lambda: ring(3, 0), tokens_three),
        (lambda: ring(1, 2), tokens_two, lambda: normalise(tokens, 0), lambda: settle(marks[1])),
        (lambda: ring(2, 1), lambda: marks.append(len(sent)), lambda: normalise(came_tokens.at[0], -1),
         lambda: normalise(came_tokens.at[2], 1), lambda: normalise(came_tokens.at[1], 2)),
        (lambda: ring(2, 2), own_block, functools.partial(distance, 1) if half > 1 else share),
        (lambda: ring(3, 1), lambda: settle(marks[2]), lambda: ring(3, 2)),
    )
    for tasks in work:
        for task in tasks:
            task()
    for k in range(2, half):
        distance(k)
    settle(marks[3])
    distance(half)
    for net in range(2):
        for core in range(2):
            columns = slice((2 * core + net) * HD, (2 * core + net + 1) * HD)
            key_values[:, columns] = total[net, :, core * HD : (core + 1) * HD].astype(BF16)


def hand_over(*refs):
    given, taken, done = refs[:3], refs[3:6], refs[6]
    copies = [pltpu.make_async_copy(a, b, done.at[k]) for k, (a, b) in enumerate(zip(given, taken))]
    for copy in copies:
        copy.start()
    for copy in copies:
        copy.wait()


def per_device(n, d_model, master, momentum, gradient, bucket_table, tokens, norm_gain):
    height = master.shape[1]
    count, width = tokens.shape
    blocks = width // HD
    rows = PACKED // n
    half = n // 2
    hbm, anywhere, vmem = (pl.BlockSpec(memory_space=m) for m in (pltpu.HBM, pl.ANY, pltpu.VMEM))
    dma = pltpu.SemaphoreType.DMA
    scratch = [
        pltpu.SMEM(bucket_table.shape, jnp.int32),
        *[pltpu.VMEM(master.shape, F32) for _ in range(3)],
        pltpu.VMEM(tokens.shape, BF16),
        pltpu.VMEM((4 * blocks, HD), F32),
        dma((6,)),
        pltpu.VMEM((8, height, HD), F32),
        pltpu.VMEM((8, height, HD), F32),
        pltpu.VMEM((4, height, HD), F32),
        pltpu.VMEM((4, height, HD), F32),
        pltpu.VMEM((2, height, HD), F32),
        pltpu.VMEM((2, PACKED, HD), F32),
        pltpu.VMEM((2, n - 1, rows, HD), F32),
        pltpu.VMEM((2, rows, HD), F32),
        pltpu.VMEM((2, n - 1, rows, HD), F32),
        pltpu.VMEM((2, PACKED, HD), F32),
        pltpu.VMEM((8, 2, height, HD), F32),
        pltpu.VMEM((2, 2, n, n, 2, height, HD), BF16),
        pltpu.VMEM((3, count, width), BF16),
        pltpu.VMEM((count, HD), F32),
        pltpu.VMEM((4 * blocks, count, HD), BF16),
        pltpu.VMEM((2, count, 2 * HD), F32),
        dma((4,)),
        dma((4,)),
        dma((3, 2, 2, n - 1)),
        dma((3, 2, 2, n - 1)),
        dma((6,)),
        dma((6,)),
        dma((2, n)),
        dma((2, n)),
        dma((2, n, 3)),
        dma((2, n, 3)),
        dma((2, 2, half, 3)),
        dma((2, 2, half, 3)),
    ]
    outs = (
        jax.ShapeDtypeStruct(master.shape, F32),
        jax.ShapeDtypeStruct(master.shape, F32),
        jax.ShapeDtypeStruct((count, 4 * HD), BF16),
    )
    made = pl.pallas_call(
        functools.partial(kernel, n, d_model),
        out_shape=outs,
        in_specs=[hbm] * 6,
        out_specs=(vmem,) * 3,
        scratch_shapes=scratch,
        compiler_params=pltpu.CompilerParams(
            collective_id=0, has_side_effects=True, vmem_limit_bytes=48 * 1024 * 1024
        ),
    )(*(
        pltpu.with_memory_space_constraint(a, pltpu.HBM)
        for a in (bucket_table, master, momentum, gradient, tokens, norm_gain.reshape(-1, HD))
    ))
    return pl.pallas_call(
        hand_over,
        out_shape=outs,
        in_specs=[vmem] * 3,
        out_specs=(hbm,) * 3,
        scratch_shapes=[dma((3,))],
        compiler_params=pltpu.CompilerParams(vmem_limit_bytes=4 * 1024 * 1024),
    )(*made)


def solution(mesh):
    n = math.isqrt(mesh.shape["dp"] // 2)
    torus = Mesh(
        mesh.devices.reshape(n, n, 2, mesh.shape["tensor"]), ("dp_0", "dp_1", "dp_2", "tensor")
    )

    def whole(*args):
        return jax.shard_map(
            functools.partial(per_device, n, args[0].shape[1]),
            mesh=torus,
            in_specs=(
                P(None, DP, "tensor"),
                P(None, DP, "tensor"),
                P(None, DP, "tensor"),
                P("tensor", None),
                P(DP, "tensor"),
                P(),
            ),
            out_specs=(P(None, DP, "tensor"), P(None, DP, "tensor"), P(DP, "tensor")),
            check_vma=False,
        )(*args)

    return whole
```

```python
import functools
import math

import jax
import jax.numpy as jnp
from jax import lax
from jax.experimental import pallas as pl
from jax.experimental.pallas import tpu as pltpu
from jax.sharding import Mesh
from jax.sharding import PartitionSpec as P

HD = 128
NS_ITERS = 3
DP = ("dp_0", "dp_1", "dp_2")

beta_momentum = 0.95
learn_rate = 0.05
first_coeff = 3.4445
cube_coeff = -4.775
fifth_coeff = 2.0315
frob_epsilon = 1e-07
rms_epsilon = 1e-05

F32 = jnp.float32
BF16 = jnp.bfloat16
Y, Z, C, X = "dp_1", "dp_0", "dp_2", "tensor"
PACKED = 2 * HD + 64


def near_first(n):
    offsets = [0]
    for k in range(1, n // 2):
        offsets += [k, -k]
    return [*offsets, n // 2]


def split(a):
    high = a.astype(BF16)
    return high, (a - high.astype(F32)).astype(BF16)


def dot(a, b):
    return jnp.dot(a, b, preferred_element_type=F32)


def dot3(a, b):
    return dot(a[0], b[0]) + (dot(a[0], b[1]) + dot(a[1], b[0]))


def kernel(n, d_model, table_in, master_in, momentum_in, gradient_in, tokens_in, gain_in, new_master,
           new_momentum, key_values, table, master, momentum, gradient, tokens, gain, load, update,
           stacked, other_rows, heads, other_heads, packed, came1, part, came2, gram, ortho, weights,
           came_tokens, squares, normed, total, pair_send, pair_recv, gram_send,
           gram_recv, token_send, token_recv, first_send, first_recv, core_send, core_recv, ring_send,
           ring_recv):
    half = n // 2
    rows = PACKED // n
    count = tokens.shape[0]
    blocks = tokens.shape[1] // HD
    height = master.shape[1]
    z, y, c, x = (lax.axis_index(a) for a in (Z, Y, C, X))
    axes = ((Y, Z), (Z, Y))
    place = {Y: y, Z: z}
    sent, ended = [], [0]

    def at(axis, offset, size):
        here = {Y: y, Z: z, X: x}[axis]
        return lax.rem(here + (offset + size), size)

    def send(src, dst, sems, to):
        copy = pltpu.make_async_remote_copy(
            src_ref=src, dst_ref=dst, send_sem=sems[0], recv_sem=sems[1],
            device_id=to, device_id_type=pl.DeviceIdType.MESH,
        )
        copy.start()
        sent.append(copy)

    def arrived(ref, sems, to):
        pltpu.make_async_remote_copy(
            src_ref=ref, dst_ref=ref, send_sem=sems[0], recv_sem=sems[1],
            device_id=to, device_id_type=pl.DeviceIdType.MESH,
        ).wait_recv()

    def settle(mark):
        for copy in sent[ended[0] : mark]:
            copy.wait_send()
        ended[0] = max(ended[0], mark)

    partner = {C: 1 - c}

    barrier = pltpu.get_barrier_semaphore()
    greeted = [partner, {X: at(X, 1, 4)}, {X: at(X, -1, 4)}]
    for axis in (Y, Z):
        greeted += [{axis: at(axis, d, n)} for d in range(1, n)]
    for device in greeted:
        pl.semaphore_signal(barrier, inc=1, device_id=device, device_id_type=pl.DeviceIdType.MESH)

    loads = [
        pltpu.make_async_copy(src, dst, load.at[k])
        for k, (src, dst) in enumerate((
            (table_in, table), (gradient_in, gradient), (momentum_in, momentum),
            (master_in, master), (tokens_in, tokens), (gain_in, gain),
        ))
    ]
    for copy in loads:
        copy.start()
    loads[0].wait()

    bucket = [table[0, i] for i in range(8)]
    position = []
    for i in range(8):
        earlier = jnp.int32(0)
        for j in range(i):
            earlier += jnp.where(bucket[j] == bucket[i], 1, 0)
        position.append(2 * bucket[i] + earlier)
    held = []
    for s in range(8):
        which = jnp.int32(0)
        for i in range(8):
            which += jnp.where(position[i] == s, i, 0)
        held.append(which)

    for copy in loads[1:4]:
        copy.wait()
    for layer in range(2):
        for slot in range(4):
            lanes = slice(slot * HD, (slot + 1) * HD)
            g = gradient[layer, :, lanes]
            m = beta_momentum * momentum[layer, :, lanes] + g
            new_momentum[layer, :, lanes] = m
            update[layer * 4 + slot] = g + beta_momentum * m
            if layer == 0:
                heads[slot] = master[0, :, lanes]
    for s in range(8):
        stacked[s] = update[held[s]]

    pl.semaphore_wait(barrier, len(greeted))

    def pair(k):
        return pair_send.at[k], pair_recv.at[k]

    send(stacked.at[pl.ds(4 * (1 - c), 4)], other_rows, pair(0), partner)
    send(heads.at[pl.ds(2 * (1 - c), 2)], other_heads, pair(1), partner)

    right, left = {X: at(X, 1, 4)}, {X: at(X, -1, 4)}
    upper, lower = pl.ds(0, count // 2), pl.ds(count // 2, count // 2)

    for copy in loads[4:]:
        copy.wait()

    def tok(k):
        return token_send.at[k], token_recv.at[k]

    send(tokens.at[upper], came_tokens.at[0, upper], tok(0), right)
    send(tokens.at[lower], came_tokens.at[2, lower], tok(1), left)
    send(tokens.at[lower], came_tokens.at[0, lower], tok(2), right)
    send(tokens.at[upper], came_tokens.at[2, upper], tok(3), left)

    arrived(other_rows, pair(0), partner)

    def chip_rows(b):
        own = jnp.concatenate([stacked[4 * c + 2 * b], stacked[4 * c + 2 * b + 1]], axis=1)
        other = jnp.concatenate([other_rows[2 * b], other_rows[2 * b + 1]], axis=1)
        return jnp.concatenate([own, other], axis=0)

    parts = ((0, 16), (16, rows))

    def lines(ref, net, chunk, p):
        low, high = parts[p]
        return ref.at[net, pl.ds(pl.multiple_of(chunk * rows + low, 8), high - low)]

    def some(ref, net, d, p):
        low, high = parts[p]
        return ref.at[net, d - 1, pl.ds(low, high - low)]

    far_first = [o % n for o in reversed(near_first(n)[1:])]

    def gsem(stage, net, p, d):
        return gram_send.at[stage, net, p, d - 1], gram_recv.at[stage, net, p, d - 1]

    r_id = lax.broadcasted_iota(jnp.int32, (HD, HD), 0)
    c_id = lax.broadcasted_iota(jnp.int32, (HD, HD), 1)
    for net in range(2):
        s = chip_rows(net)
        g = dot3(split(s.T), split(s))
        second = g[HD:, HD:]
        packed[net, 0:HD] = jnp.where(r_id <= c_id, g[:HD, :HD], second)
        packed[net, HD : 2 * HD] = g[:HD, HD:]
        diagonal = jnp.sum(jnp.where(r_id == c_id, second, 0.0), axis=0, keepdims=True)
        packed[net, 2 * HD :] = jnp.broadcast_to(diagonal, (PACKED - 2 * HD, HD))
    for p in range(2):
        for net in range(2):
            axis = axes[net][0]
            for d in far_first:
                to = at(axis, d, n)
                send(lines(packed, net, to, p), some(came1, net, d, p), gsem(0, net, p, d), {axis: to})

    def add_squares(src, fresh):
        tile = 32 if count % 32 == 0 else 16

        def body(i, _):
            r = pl.ds(pl.multiple_of(i * tile, tile), tile)
            t = jnp.zeros((tile, HD), F32) if fresh else squares[r]
            for j in range(blocks):
                v = src[r, j * HD : (j + 1) * HD].astype(F32)
                t = t + v * v
            squares[r] = t
            return 0

        lax.fori_loop(0, count // tile, body, 0)

    add_squares(tokens, True)

    for p, (low, high) in enumerate(parts):
        for net in range(2):
            axis, other = axes[net]
            for d in range(1, n):
                arrived(some(came1, net, d, p), gsem(0, net, p, d), {axis: at(axis, d, n)})
            t = lines(packed, net, place[axis], p)[...]
            for d in range(1, n):
                t = t + came1[net, d - 1, low:high]
            part[net, low:high] = t
            for d in far_first:
                send(part.at[net, pl.ds(low, high - low)], some(came2, net, d, p), gsem(1, net, p, d),
                     {other: at(other, d, n)})
    for p, (low, high) in enumerate(parts):
        for net in range(2):
            axis, other = axes[net]
            for d in range(1, n):
                arrived(some(came2, net, d, p), gsem(1, net, p, d), {other: at(other, d, n)})
            t = part[net, low:high]
            for d in range(1, n):
                t = t + came2[net, d - 1, low:high]
            own = lines(gram, net, place[axis], p)
            own[...] = t
            for d in far_first:
                send(own, own, gsem(2, net, p, d), {axis: at(axis, d, n)})

    arrived(came_tokens.at[0, upper], tok(0), right)
    send(came_tokens.at[0, upper], came_tokens.at[1, upper], tok(4), right)
    arrived(came_tokens.at[2, lower], tok(1), left)
    send(came_tokens.at[2, lower], came_tokens.at[1, lower], tok(5), left)

    for net in range(2):
        axis = axes[net][0]
        for p in range(2):
            for d in range(1, n):
                arrived(lines(gram, net, at(axis, -d, n), p), gsem(2, net, p, d), {axis: at(axis, d, n)})

    eye = jnp.where(
        lax.broadcasted_iota(jnp.int32, (2 * HD, 2 * HD), 0)
        == lax.broadcasted_iota(jnp.int32, (2 * HD, 2 * HD), 1), 1.0, 0.0
    ).astype(F32)
    step = learn_rate * math.sqrt(max(1.0, d_model / (2.0 * HD)))
    grams, ortho_rows = [], []
    for net in range(2):
        both, corner = gram[net, 0:HD], gram[net, HD : 2 * HD]
        turned = both.T
        one = jnp.where(r_id <= c_id, both, turned)
        two = jnp.where(r_id > c_id, both, jnp.where(r_id < c_id, turned, gram[net, 2 * HD : 2 * HD + 1]))
        top = jnp.concatenate([one, corner], axis=1)
        bottom = jnp.concatenate([corner.T, two], axis=1)
        g = jnp.concatenate([top, bottom], axis=0)
        trace = jnp.sum(jnp.sum(g * eye, axis=1, keepdims=True), axis=0, keepdims=True)
        scale = 1.0 / (jnp.sqrt(trace) + frob_epsilon)
        grams.append(g * (scale * scale))
        ortho_rows.append(chip_rows(net) * scale)
    for iteration in range(NS_ITERS):
        gs = [split(g) for g in grams]
        squared = [dot3(g, g) for g in gs]
        factor = [
            first_coeff * eye + (cube_coeff * g + fifth_coeff * q) for g, q in zip(grams, squared)
        ]
        fs = [split(f) for f in factor]
        if iteration + 1 < NS_ITERS:
            half_way = [dot3(f, g) for f, g in zip(fs, gs)]
            grams = [dot3(split(h), f) for h, f in zip(half_way, fs)]
            ortho_rows = [dot3(split(o), f) for o, f in zip(ortho_rows, fs)]

    for net in range(2):
        moved = dot3(split(ortho_rows[net]), fs[net]) * step
        for h in range(2):
            lanes = slice(h * HD, (h + 1) * HD)
            ortho[4 * c + 2 * net + h, c] = moved[:height, lanes]
            ortho[4 * c + 2 * net + h, 1 - c] = moved[height:, lanes]
        mine = ortho.at[pl.ds(4 * c + 2 * net, 2)]
        send(mine, mine, pair(2 + net), partner)
    arrived(other_heads, pair(1), partner)
    for net in range(2):
        arrived(ortho.at[pl.ds(4 * (1 - c) + 2 * net, 2)], pair(2 + net), partner)

    order = near_first(n)
    slot_of = {o % n: k for k, o in enumerate(order)}
    ring_axis = (Z, Y)

    near = n // 4
    groups = ((0, 1), (1, 2 * near + 1), (2 * near + 1, n))

    def rsem(net, way, s, g):
        return ring_send.at[net, way, s, g], ring_recv.at[net, way, s, g]

    def fsem(net, k):
        return first_send.at[net, k], first_recv.at[net, k]

    def sub(net, offset, g, core=c):
        low, high = groups[g]
        return weights.at[core, net, at(ring_axis[net], offset, n), pl.ds(low, high - low)]

    def piece(net, k):
        return weights.at[c, net, place[ring_axis[net]], k]

    def give(net, target, source, to):
        k = slot_of[target % n]
        send(piece(net, source), piece(net, k), fsem(net, k), {axes[net][0]: at(axes[net][0], to, n)})

    def give_near(net):
        for t in range(1, near + 1):
            give(net, t, 0, -t)
            give(net, -t, 0, t)

    def give_far(net):
        ahead, behind = slot_of[near % n], slot_of[-near % n]
        for t in range(near + 1, half):
            give(net, t, ahead, near - t)
            give(net, -t, behind, t - near)
        give(net, half, jnp.where(c == 0, ahead, behind), (2 * c - 1) * (half - near))

    def first_came(net, g):
        if groups[g][0] < groups[g][1]:
            fresh.append((net, 0, g))
        for k in range(*groups[g]):
            arrived(piece(net, k), fsem(net, k), {axes[net][0]: at(axes[net][0], 1, n)})

    def csem(net, offset, g):
        return core_send.at[net, offset % n, g], core_recv.at[net, offset % n, g]

    fresh = []

    def share():
        while fresh:
            net, offset, g = fresh.pop(0)
            moving = sub(net, offset, g)
            send(moving, moving, csem(net, offset, g), partner)

    def shared(net, offset):
        for g, (low, high) in enumerate(groups):
            if low < high:
                arrived(sub(net, offset, g, 1 - c), csem(net, offset, g), partner)

    def goes(way, s, g):
        low, high = groups[g]
        return low < high and (s + 1 < half or (way == 0) == (g == 2))

    seen = set()

    def need(net, way, s, g):
        if (net, way, s, g) in seen or not goes(way, s, g):
            return
        seen.add((net, way, s, g))
        sign = 1 if way == 0 else -1
        arrived(sub(net, -sign * (s + 1), g), rsem(net, way, s, g),
                {ring_axis[net]: at(ring_axis[net], sign, n)})
        fresh.append((net, -sign * (s + 1), g))

    def skip_one():
        for net in range(2):
            for way, sign in enumerate((1, -1)):
                if half > 2:
                    own = sub(net, 0, 0)
                    send(own, own, rsem(net, way, 1, 0),
                         {ring_axis[net]: at(ring_axis[net], 2 * sign, n)})

    def ring(s, g):
        if s >= half:
            return
        for net in range(2):
            for way, sign in enumerate((1, -1)):
                if goes(way, s, g):
                    if s > 0:
                        need(net, way, s - 1, g)
                    if half > 2 and (s, g) == (1, 0):
                        continue
                    moving = sub(net, -sign * s, g)
                    send(moving, moving, rsem(net, way, s, g),
                         {ring_axis[net]: at(ring_axis[net], sign, n)})
        share()

    marks = [len(sent)]
    for net in range(2):
        where = jnp.where(c == 0, position[net], position[2 + net])
        block = place[ring_axis[net]]
        weights[c, net, block, 0, c] = (heads[2 * c + net] - ortho[where, c]).astype(BF16)
        weights[c, net, block, 0, 1 - c] = (other_heads[net] - ortho[where, 1 - c]).astype(BF16)
        give_near(net)
        fresh.append((net, 0, 0))
    ring(0, 0)
    skip_one()
    for net in range(2):
        first_came(net, 1)
        give_far(net)
    ring(0, 1)
    marks.append(len(sent))

    for i in range(8):
        lanes = slice((i % 4) * HD, (i % 4 + 1) * HD)
        new_master[i // 4, :, lanes] = master[i // 4, :, lanes] - ortho[position[i], c]
    ring(1, 0)
    for net in range(2):
        first_came(net, 2)
    ring(0, 2)
    ring(2, 0)

    def inverse_rms():
        mean = jnp.sum(squares[...], axis=1, keepdims=True) / d_model
        squares[...] = jnp.broadcast_to(lax.rsqrt(mean + rms_epsilon), squares.shape)

    def normalise(src, offset):
        tile = 32 if count % 32 == 0 else 16
        first = at(X, offset, 4) * blocks

        def body(i, _):
            r = pl.ds(pl.multiple_of(i * tile, tile), tile)
            inverse = squares[r]
            for j in range(blocks):
                v = src[r, j * HD : (j + 1) * HD].astype(F32)
                v = v * inverse * gain[pl.ds(first + j, 1), :]
                normed[first + j, r] = v.astype(BF16)
            return 0

        lax.fori_loop(0, count // tile, body, 0)
    def multiply(net, offset, first=False):
        shared(net, offset)
        block = at(ring_axis[net], offset, n)
        axis = axes[net][0]
        wide = []
        for o in order:
            across = at(axis, o, n)
            wide.append(normed[block * n + across if net == 0 else across * n + block])
        tall = [weights[core, net, block].reshape(n * HD, HD) for core in range(2)]
        product = dot(jnp.concatenate(wide, axis=1), jnp.concatenate(tall, axis=1))
        total[net] = product if first else total[net] + product

    def tokens_one():
        arrived(came_tokens.at[0, lower], tok(2), right)
        add_squares(came_tokens.at[0], False)

    def tokens_three():
        arrived(came_tokens.at[2, upper], tok(3), left)
        add_squares(came_tokens.at[2], False)

    def tokens_two():
        arrived(came_tokens.at[1, upper], tok(4), right)
        arrived(came_tokens.at[1, lower], tok(5), left)
        add_squares(came_tokens.at[1], False)
        inverse_rms()

    def own_block():
        for net in range(2):
            multiply(net, 0, True)

    def distance(k):
        for net in range(2):
            for g in range(3):
                for way in range(2):
                    need(net, way, k - 1, g)
        share()
        if k == half:
            settle(len(sent))
        for net in range(2):
            multiply(net, k)
            if k < half:
                multiply(net, -k)

    work = (
        (lambda: ring(1, 1), tokens_one, lambda: settle(marks[0]), lambda: marks.append(len(sent))),
        (lambda: ring(3, 0), tokens_three),
        (lambda: ring(1, 2), tokens_two, lambda: normalise(tokens, 0),
         lambda: normalise(came_tokens.at[0], -1)),
        (lambda: ring(2, 1), lambda: marks.append(len(sent)), lambda: normalise(came_tokens.at[2], 1),
         lambda: normalise(came_tokens.at[1], 2)),
        (lambda: ring(2, 2), own_block, lambda: settle(marks[1])),
        (lambda: ring(3, 1), functools.partial(distance, 1) if half > 1 else share),
        (lambda: ring(3, 2), lambda: settle(marks[2])),
    )
    for tasks in work:
        for task in tasks:
            task()
    for k in range(2, half):
        distance(k)
    settle(marks[3])
    distance(half)
    for net in range(2):
        for core in range(2):
            columns = slice((2 * core + net) * HD, (2 * core + net + 1) * HD)
            key_values[:, columns] = total[net, :, core * HD : (core + 1) * HD].astype(BF16)


def hand_over(*refs):
    given, taken, done = refs[:3], refs[3:6], refs[6]
    copies = [pltpu.make_async_copy(a, b, done.at[k]) for k, (a, b) in enumerate(zip(given, taken))]
    for copy in copies:
        copy.start()
    for copy in copies:
        copy.wait()


def per_device(n, d_model, master, momentum, gradient, bucket_table, tokens, norm_gain):
    height = master.shape[1]
    count, width = tokens.shape
    blocks = width // HD
    rows = PACKED // n
    half = n // 2
    hbm, anywhere, vmem = (pl.BlockSpec(memory_space=m) for m in (pltpu.HBM, pl.ANY, pltpu.VMEM))
    dma = pltpu.SemaphoreType.DMA
    scratch = [
        pltpu.SMEM(bucket_table.shape, jnp.int32),
        *[pltpu.VMEM(master.shape, F32) for _ in range(3)],
        pltpu.VMEM(tokens.shape, BF16),
        pltpu.VMEM((4 * blocks, HD), F32),
        dma((6,)),
        pltpu.VMEM((8, height, HD), F32),
        pltpu.VMEM((8, height, HD), F32),
        pltpu.VMEM((4, height, HD), F32),
        pltpu.VMEM((4, height, HD), F32),
        pltpu.VMEM((2, height, HD), F32),
        pltpu.VMEM((2, PACKED, HD), F32),
        pltpu.VMEM((2, n - 1, rows, HD), F32),
        pltpu.VMEM((2, rows, HD), F32),
        pltpu.VMEM((2, n - 1, rows, HD), F32),
        pltpu.VMEM((2, PACKED, HD), F32),
        pltpu.VMEM((8, 2, height, HD), F32),
        pltpu.VMEM((2, 2, n, n, 2, height, HD), BF16),
        pltpu.VMEM((3, count, width), BF16),
        pltpu.VMEM((count, HD), F32),
        pltpu.VMEM((4 * blocks, count, HD), BF16),
        pltpu.VMEM((2, count, 2 * HD), F32),
        dma((4,)),
        dma((4,)),
        dma((3, 2, 2, n - 1)),
        dma((3, 2, 2, n - 1)),
        dma((6,)),
        dma((6,)),
        dma((2, n)),
        dma((2, n)),
        dma((2, n, 3)),
        dma((2, n, 3)),
        dma((2, 2, half, 3)),
        dma((2, 2, half, 3)),
    ]
    outs = (
        jax.ShapeDtypeStruct(master.shape, F32),
        jax.ShapeDtypeStruct(master.shape, F32),
        jax.ShapeDtypeStruct((count, 4 * HD), BF16),
    )
    made = pl.pallas_call(
        functools.partial(kernel, n, d_model),
        out_shape=outs,
        in_specs=[hbm] * 6,
        out_specs=(vmem,) * 3,
        scratch_shapes=scratch,
        compiler_params=pltpu.CompilerParams(
            collective_id=0, has_side_effects=True, vmem_limit_bytes=48 * 1024 * 1024
        ),
    )(*(
        pltpu.with_memory_space_constraint(a, pltpu.HBM)
        for a in (bucket_table, master, momentum, gradient, tokens, norm_gain.reshape(-1, HD))
    ))
    return pl.pallas_call(
        hand_over,
        out_shape=outs,
        in_specs=[vmem] * 3,
        out_specs=(hbm,) * 3,
        scratch_shapes=[dma((3,))],
        compiler_params=pltpu.CompilerParams(vmem_limit_bytes=4 * 1024 * 1024),
    )(*made)


def solution(mesh):
    n = math.isqrt(mesh.shape["dp"] // 2)
    torus = Mesh(
        mesh.devices.reshape(n, n, 2, mesh.shape["tensor"]), ("dp_0", "dp_1", "dp_2", "tensor")
    )

    def whole(*args):
        return jax.shard_map(
            functools.partial(per_device, n, args[0].shape[1]),
            mesh=torus,
            in_specs=(
                P(None, DP, "tensor"),
                P(None, DP, "tensor"),
                P(None, DP, "tensor"),
                P("tensor", None),
                P(DP, "tensor"),
                P(),
            ),
            out_specs=(P(None, DP, "tensor"), P(None, DP, "tensor"), P(DP, "tensor")),
            check_vma=False,
        )(*args)

    return whole
```

```python
import functools
import math

import jax
import jax.numpy as jnp
from jax import lax
from jax.experimental import pallas as pl
from jax.experimental.pallas import tpu as pltpu
from jax.sharding import Mesh
from jax.sharding import PartitionSpec as P

HD = 128
NS_ITERS = 3
DP = ("dp_0", "dp_1", "dp_2")

beta_momentum = 0.95
learn_rate = 0.05
first_coeff = 3.4445
cube_coeff = -4.775
fifth_coeff = 2.0315
frob_epsilon = 1e-07
rms_epsilon = 1e-05

F32 = jnp.float32
BF16 = jnp.bfloat16
Y, Z, C, X = "dp_1", "dp_0", "dp_2", "tensor"
PACKED = 2 * HD + 64


def near_first(n):
    offsets = [0]
    for k in range(1, n // 2):
        offsets += [k, -k]
    return [*offsets, n // 2]


def split(a):
    high = a.astype(BF16)
    return high, (a - high.astype(F32)).astype(BF16)


def dot(a, b):
    return jnp.dot(a, b, preferred_element_type=F32)


def dot3(a, b):
    return dot(a[0], b[0]) + (dot(a[0], b[1]) + dot(a[1], b[0]))


def kernel(n, d_model, table_in, master_in, momentum_in, gradient_in, tokens_in, gain_in, new_master,
           new_momentum, key_values, table, master, momentum, gradient, tokens, gain, load, update,
           stacked, other_rows, heads, other_heads, packed, came1, part, came2, gram, ortho, weights,
           came_tokens, squares, normed, total, pair_send, pair_recv, gram_send,
           gram_recv, token_send, token_recv, first_send, first_recv, core_send, core_recv, ring_send,
           ring_recv):
    half = n // 2
    rows = PACKED // n
    count = tokens.shape[0]
    blocks = tokens.shape[1] // HD
    height = master.shape[1]
    z, y, c, x = (lax.axis_index(a) for a in (Z, Y, C, X))
    axes = ((Y, Z), (Z, Y))
    place = {Y: y, Z: z}
    sent, ended = [], [0]

    def at(axis, offset, size):
        here = {Y: y, Z: z, X: x}[axis]
        return lax.rem(here + (offset + size), size)

    def send(src, dst, sems, to):
        copy = pltpu.make_async_remote_copy(
            src_ref=src, dst_ref=dst, send_sem=sems[0], recv_sem=sems[1],
            device_id=to, device_id_type=pl.DeviceIdType.MESH,
        )
        copy.start()
        sent.append(copy)

    def arrived(ref, sems, to):
        pltpu.make_async_remote_copy(
            src_ref=ref, dst_ref=ref, send_sem=sems[0], recv_sem=sems[1],
            device_id=to, device_id_type=pl.DeviceIdType.MESH,
        ).wait_recv()

    def settle(mark):
        for copy in sent[ended[0] : mark]:
            copy.wait_send()
        ended[0] = max(ended[0], mark)

    partner = {C: 1 - c}

    barrier = pltpu.get_barrier_semaphore()
    greeted = [partner, {X: at(X, 1, 4)}, {X: at(X, -1, 4)}]
    for axis in (Y, Z):
        greeted += [{axis: at(axis, d, n)} for d in range(1, n)]
    for device in greeted:
        pl.semaphore_signal(barrier, inc=1, device_id=device, device_id_type=pl.DeviceIdType.MESH)

    loads = [
        pltpu.make_async_copy(src, dst, load.at[k])
        for k, (src, dst) in enumerate((
            (table_in, table), (gradient_in, gradient), (momentum_in, momentum),
            (master_in, master), (tokens_in, tokens), (gain_in, gain),
        ))
    ]
    for copy in loads:
        copy.start()
    loads[0].wait()

    bucket = [table[0, i] for i in range(8)]
    position = []
    for i in range(8):
        earlier = jnp.int32(0)
        for j in range(i):
            earlier += jnp.where(bucket[j] == bucket[i], 1, 0)
        position.append(2 * bucket[i] + earlier)
    held = []
    for s in range(8):
        which = jnp.int32(0)
        for i in range(8):
            which += jnp.where(position[i] == s, i, 0)
        held.append(which)

    for copy in loads[1:4]:
        copy.wait()
    for layer in range(2):
        for slot in range(4):
            lanes = slice(slot * HD, (slot + 1) * HD)
            g = gradient[layer, :, lanes]
            m = beta_momentum * momentum[layer, :, lanes] + g
            new_momentum[layer, :, lanes] = m
            update[layer * 4 + slot] = g + beta_momentum * m
            if layer == 0:
                heads[slot] = master[0, :, lanes]
    for s in range(8):
        stacked[s] = update[held[s]]

    pl.semaphore_wait(barrier, len(greeted))

    def pair(k):
        return pair_send.at[k], pair_recv.at[k]

    send(stacked.at[pl.ds(4 * (1 - c), 4)], other_rows, pair(0), partner)
    send(heads.at[pl.ds(2 * (1 - c), 2)], other_heads, pair(1), partner)

    right, left = {X: at(X, 1, 4)}, {X: at(X, -1, 4)}
    upper, lower = pl.ds(0, count // 2), pl.ds(count // 2, count // 2)

    for copy in loads[4:]:
        copy.wait()

    def tok(k):
        return token_send.at[k], token_recv.at[k]

    send(tokens.at[upper], came_tokens.at[0, upper], tok(0), right)
    send(tokens.at[lower], came_tokens.at[2, lower], tok(1), left)
    send(tokens.at[lower], came_tokens.at[0, lower], tok(2), right)
    send(tokens.at[upper], came_tokens.at[2, upper], tok(3), left)

    arrived(other_rows, pair(0), partner)

    def chip_rows(b):
        own = jnp.concatenate([stacked[4 * c + 2 * b], stacked[4 * c + 2 * b + 1]], axis=1)
        other = jnp.concatenate([other_rows[2 * b], other_rows[2 * b + 1]], axis=1)
        return jnp.concatenate([own, other], axis=0)

    parts = ((0, 16), (16, rows))

    def lines(ref, net, chunk, p):
        low, high = parts[p]
        return ref.at[net, pl.ds(pl.multiple_of(chunk * rows + low, 8), high - low)]

    def some(ref, net, d, p):
        low, high = parts[p]
        return ref.at[net, d - 1, pl.ds(low, high - low)]

    far_first = [o % n for o in reversed(near_first(n)[1:])]

    def gsem(stage, net, p, d):
        return gram_send.at[stage, net, p, d - 1], gram_recv.at[stage, net, p, d - 1]

    r_id = lax.broadcasted_iota(jnp.int32, (HD, HD), 0)
    c_id = lax.broadcasted_iota(jnp.int32, (HD, HD), 1)
    for net in range(2):
        s = chip_rows(net)
        g = dot3(split(s.T), split(s))
        second = g[HD:, HD:]
        packed[net, 0:HD] = jnp.where(r_id <= c_id, g[:HD, :HD], second)
        packed[net, HD : 2 * HD] = g[:HD, HD:]
        diagonal = jnp.sum(jnp.where(r_id == c_id, second, 0.0), axis=0, keepdims=True)
        packed[net, 2 * HD :] = jnp.broadcast_to(diagonal, (PACKED - 2 * HD, HD))
    for p in range(2):
        for net in range(2):
            axis = axes[net][0]
            for d in far_first:
                to = at(axis, d, n)
                send(lines(packed, net, to, p), some(came1, net, d, p), gsem(0, net, p, d), {axis: to})

    def add_squares(src, fresh):
        tile = 32 if count % 32 == 0 else 16

        def body(i, _):
            r = pl.ds(pl.multiple_of(i * tile, tile), tile)
            t = jnp.zeros((tile, HD), F32) if fresh else squares[r]
            for j in range(blocks):
                v = src[r, j * HD : (j + 1) * HD].astype(F32)
                t = t + v * v
            squares[r] = t
            return 0

        lax.fori_loop(0, count // tile, body, 0)

    add_squares(tokens, True)

    for p, (low, high) in enumerate(parts):
        for net in range(2):
            axis, other = axes[net]
            for d in range(1, n):
                arrived(some(came1, net, d, p), gsem(0, net, p, d), {axis: at(axis, d, n)})
            t = lines(packed, net, place[axis], p)[...]
            for d in range(1, n):
                t = t + came1[net, d - 1, low:high]
            part[net, low:high] = t
            for d in far_first:
                send(part.at[net, pl.ds(low, high - low)], some(came2, net, d, p), gsem(1, net, p, d),
                     {other: at(other, d, n)})
    for p, (low, high) in enumerate(parts):
        for net in range(2):
            axis, other = axes[net]
            for d in range(1, n):
                arrived(some(came2, net, d, p), gsem(1, net, p, d), {other: at(other, d, n)})
            t = part[net, low:high]
            for d in range(1, n):
                t = t + came2[net, d - 1, low:high]
            own = lines(gram, net, place[axis], p)
            own[...] = t
            for d in far_first:
                send(own, own, gsem(2, net, p, d), {axis: at(axis, d, n)})

    arrived(came_tokens.at[0, upper], tok(0), right)
    send(came_tokens.at[0, upper], came_tokens.at[1, upper], tok(4), right)
    arrived(came_tokens.at[2, lower], tok(1), left)
    send(came_tokens.at[2, lower], came_tokens.at[1, lower], tok(5), left)

    for net in range(2):
        axis = axes[net][0]
        for p in range(2):
            for d in range(1, n):
                arrived(lines(gram, net, at(axis, -d, n), p), gsem(2, net, p, d), {axis: at(axis, d, n)})

    eye = jnp.where(
        lax.broadcasted_iota(jnp.int32, (2 * HD, 2 * HD), 0)
        == lax.broadcasted_iota(jnp.int32, (2 * HD, 2 * HD), 1), 1.0, 0.0
    ).astype(F32)
    step = learn_rate * math.sqrt(max(1.0, d_model / (2.0 * HD)))
    grams, ortho_rows = [], []
    for net in range(2):
        both, corner = gram[net, 0:HD], gram[net, HD : 2 * HD]
        turned = both.T
        one = jnp.where(r_id <= c_id, both, turned)
        two = jnp.where(r_id > c_id, both, jnp.where(r_id < c_id, turned, gram[net, 2 * HD : 2 * HD + 1]))
        top = jnp.concatenate([one, corner], axis=1)
        bottom = jnp.concatenate([corner.T, two], axis=1)
        g = jnp.concatenate([top, bottom], axis=0)
        trace = jnp.sum(jnp.sum(g * eye, axis=1, keepdims=True), axis=0, keepdims=True)
        scale = 1.0 / (jnp.sqrt(trace) + frob_epsilon)
        grams.append(g * (scale * scale))
        ortho_rows.append(chip_rows(net) * scale)
    for iteration in range(NS_ITERS):
        gs = [split(g) for g in grams]
        squared = [dot3(g, g) for g in gs]
        factor = [
            first_coeff * eye + (cube_coeff * g + fifth_coeff * q) for g, q in zip(grams, squared)
        ]
        fs = [split(f) for f in factor]
        if iteration + 1 < NS_ITERS:
            half_way = [dot3(f, g) for f, g in zip(fs, gs)]
            grams = [dot3(split(h), f) for h, f in zip(half_way, fs)]
            ortho_rows = [dot3(split(o), f) for o, f in zip(ortho_rows, fs)]

    for net in range(2):
        moved = dot3(split(ortho_rows[net]), fs[net]) * step
        for h in range(2):
            lanes = slice(h * HD, (h + 1) * HD)
            ortho[4 * c + 2 * net + h, c] = moved[:height, lanes]
            ortho[4 * c + 2 * net + h, 1 - c] = moved[height:, lanes]
        mine = ortho.at[pl.ds(4 * c + 2 * net, 2)]
        send(mine, mine, pair(2 + net), partner)
    arrived(other_heads, pair(1), partner)
    for net in range(2):
        arrived(ortho.at[pl.ds(4 * (1 - c) + 2 * net, 2)], pair(2 + net), partner)

    order = near_first(n)
    slot_of = {o % n: k for k, o in enumerate(order)}
    ring_axis = (Z, Y)

    near = n // 4
    groups = ((0, 1), (1, 2 * near + 1), (2 * near + 1, n))

    def rsem(net, way, s, g):
        return ring_send.at[net, way, s, g], ring_recv.at[net, way, s, g]

    def fsem(net, k):
        return first_send.at[net, k], first_recv.at[net, k]

    def sub(net, offset, g, core=c):
        low, high = groups[g]
        return weights.at[core, net, at(ring_axis[net], offset, n), pl.ds(low, high - low)]

    def piece(net, k):
        return weights.at[c, net, place[ring_axis[net]], k]

    def give(net, target, source, to):
        k = slot_of[target % n]
        send(piece(net, source), piece(net, k), fsem(net, k), {axes[net][0]: at(axes[net][0], to, n)})

    def give_near(net):
        for t in range(1, near + 1):
            give(net, t, 0, -t)
            give(net, -t, 0, t)

    def give_far(net):
        ahead, behind = slot_of[near % n], slot_of[-near % n]
        for t in range(near + 1, half):
            give(net, t, ahead, near - t)
            give(net, -t, behind, t - near)
        give(net, half, jnp.where(c == 0, ahead, behind), (2 * c - 1) * (half - near))

    def first_came(net, g):
        if groups[g][0] < groups[g][1]:
            fresh.append((net, 0, g))
        for k in range(*groups[g]):
            arrived(piece(net, k), fsem(net, k), {axes[net][0]: at(axes[net][0], 1, n)})

    def csem(net, offset, g):
        return core_send.at[net, offset % n, g], core_recv.at[net, offset % n, g]

    fresh, came = [], {}
    used = [g for g in range(3) if groups[g][0] < groups[g][1]]

    def block_of(net, offset, core):
        return weights.at[core, net, at(ring_axis[net], offset, n)]

    def share():
        while fresh:
            net, offset, g = fresh.pop(0)
            if offset % n == half:
                moving = sub(net, offset, g)
                send(moving, moving, csem(net, offset, g), partner)
                continue
            came[net, offset] = came.get((net, offset), 0) + 1
            if came[net, offset] == len(used):
                moving = block_of(net, offset, c)
                send(moving, moving, csem(net, offset, 0), partner)

    def shared(net, offset):
        if offset % n != half:
            arrived(block_of(net, offset, 1 - c), csem(net, offset, 0), partner)
            return
        for g in used:
            arrived(sub(net, offset, g, 1 - c), csem(net, offset, g), partner)

    def goes(way, s, g):
        low, high = groups[g]
        return low < high and (s + 1 < half or (way == 0) == (g == 2))

    seen = set()

    def need(net, way, s, g):
        if (net, way, s, g) in seen or not goes(way, s, g):
            return
        seen.add((net, way, s, g))
        sign = 1 if way == 0 else -1
        arrived(sub(net, -sign * (s + 1), g), rsem(net, way, s, g),
                {ring_axis[net]: at(ring_axis[net], sign, n)})
        fresh.append((net, -sign * (s + 1), g))

    def skip_one():
        for net in range(2):
            for way, sign in enumerate((1, -1)):
                if half > 2:
                    own = sub(net, 0, 0)
                    send(own, own, rsem(net, way, 1, 0),
                         {ring_axis[net]: at(ring_axis[net], 2 * sign, n)})

    def ring(s, g):
        if s >= half:
            return
        for net in range(2):
            for way, sign in enumerate((1, -1)):
                if goes(way, s, g):
                    if s > 0:
                        need(net, way, s - 1, g)
                    if half > 2 and (s, g) == (1, 0):
                        continue
                    moving = sub(net, -sign * s, g)
                    send(moving, moving, rsem(net, way, s, g),
                         {ring_axis[net]: at(ring_axis[net], sign, n)})
        share()

    marks = [len(sent)]
    for net in range(2):
        where = jnp.where(c == 0, position[net], position[2 + net])
        block = place[ring_axis[net]]
        weights[c, net, block, 0, c] = (heads[2 * c + net] - ortho[where, c]).astype(BF16)
        weights[c, net, block, 0, 1 - c] = (other_heads[net] - ortho[where, 1 - c]).astype(BF16)
        give_near(net)
        fresh.append((net, 0, 0))
    ring(0, 0)
    skip_one()
    for net in range(2):
        first_came(net, 1)
        give_far(net)
    ring(0, 1)
    marks.append(len(sent))

    for i in range(8):
        lanes = slice((i % 4) * HD, (i % 4 + 1) * HD)
        new_master[i // 4, :, lanes] = master[i // 4, :, lanes] - ortho[position[i], c]
    ring(1, 0)
    for net in range(2):
        first_came(net, 2)
    ring(0, 2)
    ring(2, 0)

    def inverse_rms():
        mean = jnp.sum(squares[...], axis=1, keepdims=True) / d_model
        squares[...] = jnp.broadcast_to(lax.rsqrt(mean + rms_epsilon), squares.shape)

    def normalise(src, offset):
        tile = 32 if count % 32 == 0 else 16
        first = at(X, offset, 4) * blocks

        def body(i, _):
            r = pl.ds(pl.multiple_of(i * tile, tile), tile)
            inverse = squares[r]
            for j in range(blocks):
                v = src[r, j * HD : (j + 1) * HD].astype(F32)
                v = v * inverse * gain[pl.ds(first + j, 1), :]
                normed[first + j, r] = v.astype(BF16)
            return 0

        lax.fori_loop(0, count // tile, body, 0)
    def multiply(net, offset, first=False):
        shared(net, offset)
        block = at(ring_axis[net], offset, n)
        axis = axes[net][0]
        wide = []
        for o in order:
            across = at(axis, o, n)
            wide.append(normed[block * n + across if net == 0 else across * n + block])
        tall = [weights[core, net, block].reshape(n * HD, HD) for core in range(2)]
        product = dot(jnp.concatenate(wide, axis=1), jnp.concatenate(tall, axis=1))
        total[net] = product if first else total[net] + product

    def tokens_one():
        arrived(came_tokens.at[0, lower], tok(2), right)
        add_squares(came_tokens.at[0], False)

    def tokens_three():
        arrived(came_tokens.at[2, upper], tok(3), left)
        add_squares(came_tokens.at[2], False)

    def tokens_two():
        arrived(came_tokens.at[1, upper], tok(4), right)
        arrived(came_tokens.at[1, lower], tok(5), left)
        add_squares(came_tokens.at[1], False)
        inverse_rms()

    def own_block():
        for net in range(2):
            multiply(net, 0, True)

    def distance(k):
        for net in range(2):
            for g in range(3):
                for way in range(2):
                    need(net, way, k - 1, g)
        share()
        if k == half:
            settle(len(sent))
        for net in range(2):
            multiply(net, k)
            if k < half:
                multiply(net, -k)

    work = (
        (lambda: ring(1, 1), tokens_one, lambda: settle(marks[0]), lambda: marks.append(len(sent))),
        (lambda: ring(3, 0), tokens_three),
        (lambda: ring(1, 2), tokens_two, lambda: normalise(tokens, 0), lambda: settle(marks[1])),
        (lambda: ring(2, 1), lambda: marks.append(len(sent)), lambda: normalise(came_tokens.at[0], -1),
         lambda: normalise(came_tokens.at[2], 1), lambda: normalise(came_tokens.at[1], 2)),
        (lambda: ring(2, 2), own_block, functools.partial(distance, 1) if half > 1 else share),
        (lambda: ring(3, 1), lambda: settle(marks[2]), lambda: ring(3, 2)),
    )
    for tasks in work:
        for task in tasks:
            task()
    for k in range(2, half):
        distance(k)
    settle(marks[3])
    distance(half)
    for net in range(2):
        for core in range(2):
            columns = slice((2 * core + net) * HD, (2 * core + net + 1) * HD)
            key_values[:, columns] = total[net, :, core * HD : (core + 1) * HD].astype(BF16)


def hand_over(*refs):
    given, taken, done = refs[:3], refs[3:6], refs[6]
    copies = [pltpu.make_async_copy(a, b, done.at[k]) for k, (a, b) in enumerate(zip(given, taken))]
    for copy in copies:
        copy.start()
    for copy in copies:
        copy.wait()


def per_device(n, d_model, master, momentum, gradient, bucket_table, tokens, norm_gain):
    height = master.shape[1]
    count, width = tokens.shape
    blocks = width // HD
    rows = PACKED // n
    half = n // 2
    hbm, anywhere, vmem = (pl.BlockSpec(memory_space=m) for m in (pltpu.HBM, pl.ANY, pltpu.VMEM))
    dma = pltpu.SemaphoreType.DMA
    scratch = [
        pltpu.SMEM(bucket_table.shape, jnp.int32),
        *[pltpu.VMEM(master.shape, F32) for _ in range(3)],
        pltpu.VMEM(tokens.shape, BF16),
        pltpu.VMEM((4 * blocks, HD), F32),
        dma((6,)),
        pltpu.VMEM((8, height, HD), F32),
        pltpu.VMEM((8, height, HD), F32),
        pltpu.VMEM((4, height, HD), F32),
        pltpu.VMEM((4, height, HD), F32),
        pltpu.VMEM((2, height, HD), F32),
        pltpu.VMEM((2, PACKED, HD), F32),
        pltpu.VMEM((2, n - 1, rows, HD), F32),
        pltpu.VMEM((2, rows, HD), F32),
        pltpu.VMEM((2, n - 1, rows, HD), F32),
        pltpu.VMEM((2, PACKED, HD), F32),
        pltpu.VMEM((8, 2, height, HD), F32),
        pltpu.VMEM((2, 2, n, n, 2, height, HD), BF16),
        pltpu.VMEM((3, count, width), BF16),
        pltpu.VMEM((count, HD), F32),
        pltpu.VMEM((4 * blocks, count, HD), BF16),
        pltpu.VMEM((2, count, 2 * HD), F32),
        dma((4,)),
        dma((4,)),
        dma((3, 2, 2, n - 1)),
        dma((3, 2, 2, n - 1)),
        dma((6,)),
        dma((6,)),
        dma((2, n)),
        dma((2, n)),
        dma((2, n, 3)),
        dma((2, n, 3)),
        dma((2, 2, half, 3)),
        dma((2, 2, half, 3)),
    ]
    outs = (
        jax.ShapeDtypeStruct(master.shape, F32),
        jax.ShapeDtypeStruct(master.shape, F32),
        jax.ShapeDtypeStruct((count, 4 * HD), BF16),
    )
    made = pl.pallas_call(
        functools.partial(kernel, n, d_model),
        out_shape=outs,
        in_specs=[hbm] * 6,
        out_specs=(vmem,) * 3,
        scratch_shapes=scratch,
        compiler_params=pltpu.CompilerParams(
            collective_id=0, has_side_effects=True, vmem_limit_bytes=48 * 1024 * 1024
        ),
    )(*(
        pltpu.with_memory_space_constraint(a, pltpu.HBM)
        for a in (bucket_table, master, momentum, gradient, tokens, norm_gain.reshape(-1, HD))
    ))
    return pl.pallas_call(
        hand_over,
        out_shape=outs,
        in_specs=[vmem] * 3,
        out_specs=(hbm,) * 3,
        scratch_shapes=[dma((3,))],
        compiler_params=pltpu.CompilerParams(vmem_limit_bytes=4 * 1024 * 1024),
    )(*made)


def solution(mesh):
    n = math.isqrt(mesh.shape["dp"] // 2)
    torus = Mesh(
        mesh.devices.reshape(n, n, 2, mesh.shape["tensor"]), ("dp_0", "dp_1", "dp_2", "tensor")
    )

    def whole(*args):
        return jax.shard_map(
            functools.partial(per_device, n, args[0].shape[1]),
            mesh=torus,
            in_specs=(
                P(None, DP, "tensor"),
                P(None, DP, "tensor"),
                P(None, DP, "tensor"),
                P("tensor", None),
                P(DP, "tensor"),
                P(),
            ),
            out_specs=(P(None, DP, "tensor"), P(None, DP, "tensor"), P(DP, "tensor")),
            check_vma=False,
        )(*args)

    return whole
```
